256 devices in a mesh: ctx: 64 (over y, z, core), head: 4 (over x).
Axes of the slice: x: 4, y: 4, z: 8, core: 2. Of those that a mesh axis runs over, the one named last changes fastest.
Arguments:
- queries: bfloat16 [16384, 64, 128], P('ctx', 'head'), may hold values from -120 to 120
- keys: bfloat16 [16384, 8, 128], P('ctx', 'head'), may hold values from -7 to 7
- values: bfloat16 [16384, 8, 128], P('ctx', 'head'), may hold values from -6 to 6
- doc_lengths: int32 [32], replicated, may hold values from 1 to 1280, 16384 in all
Outputs:
- attended: bfloat16 [16384, 64, 128], P(('ctx', 'head'))
The draws below stay inside these ranges and needn't reach their ends.
Inputs may be any that keep to these rules, and one draw needn't show every extreme that they name: `doc_lengths`: the lengths sum to 16384; the longest is exactly 1280.
All inputs are finite; a program needn't handle non-finite values.
Results may differ from the reference program's by a relative error of at most 0.005.
Values may be sent and summed in bfloat16 or wider, within the bound.
A program may use at most 64 MiB of HBM per device.

```python
import math
import jax
import jax.numpy as jnp
import numpy as np
from jax import lax

HQ = 64
KEY_HEADS = 8
HEAD_WIDTH = 128
LOCAL_TOKENS = 256
REACH = 5
QUERY_PER_KEY = 8
PACKED_TOKENS = 16384
DOC_MOST = 1280
DOCS = 32


def base_keys(key):
    return jax.random.truncated_normal(key, -6.0, 6.0, (PACKED_TOKENS, KEY_HEADS, HEAD_WIDTH), jnp.float32)


def draw_keys(key, part):
    shared = base_keys(key)
    return shared.astype(jnp.bfloat16)


def draw_queries(key, part):
    key = jax.random.fold_in(key, 7)
    drawn = jax.random.truncated_normal(key, -6.0, 6.0, (PACKED_TOKENS, HQ, HEAD_WIDTH), jnp.float32)
    return drawn.astype(jnp.bfloat16)


def block_levels(own_key, dims, shards, smallest, largest):
    gain, own = 1.0, jax.random.fold_in(own_key, 6)
    for axis_at, parts in shards:
        heights = jnp.exp(jax.random.uniform(jax.random.fold_in(own, axis_at), (parts,), jnp.float32, smallest / len(shards), largest / len(shards)))
        gain = gain * jnp.repeat(heights, dims[axis_at] // parts).reshape([-1 if axis == axis_at else 1 for axis in range(len(dims))])
    return gain


def length_profile(count, total, most, lean):
    loads = [(1 << 20) // math.isqrt(standing ** lean) + 1 for standing in range(2, count + 1)]
    surplus, counts = total - most - (count - 1), [1] * (count - 1)
    while surplus > 0:
        candidates = [i for i in range(count - 1) if counts[i] < most]
        mass, left = sum([loads[i] for i in candidates]), surplus
        for i in candidates:
            addition = min(most - counts[i], max(1, left * loads[i] // mass), surplus)
            counts[i] = counts[i] + addition
            surplus = surplus - addition
    return np.array([most] + counts)


def uneven(stream_key, number_of, total, reach, lean):
    if number_of == 2:
        one = jax.random.randint(stream_key, (), max(1, total - reach), min(reach, total - 1) + 1)
        return jnp.stack([one, total - one])
    lengths = jnp.asarray(length_profile(number_of, total, reach, lean), jnp.int32)
    twos = (number_of - 1) // 2
    giver, receiver = lengths[1:1 + 2 * twos:2], lengths[2:2 + 2 * twos:2]
    room = jnp.minimum(giver - 1, reach - receiver)
    shifted = jax.random.randint(jax.random.fold_in(stream_key, 1), (twos,), 0, 1 << 20) % (room + 1)
    lengths = lengths.at[1:1 + 2 * twos:2].set(giver - shifted).at[2:2 + 2 * twos:2].set(receiver + shifted)
    return lengths[jax.random.permutation(jax.random.fold_in(stream_key, 2), number_of)]


def gaussian(rng, shape, width, most, cuts=(), kind=jnp.bfloat16):
    level = block_levels(rng, shape, cuts, -0.22, 0.18) if cuts else 1.0
    array = jax.random.normal(rng, shape, jnp.float32) * width * level
    return jnp.minimum(jnp.maximum(array, -most), most).astype(kind)


def setup_inputs(seed: int = 0) -> dict:
    key_of = jax.random.split(jax.random.key(seed), 5)
    return {
        "queries": draw_queries(jax.random.fold_in(key_of[4], 71), 0),
        "keys": draw_keys(jax.random.fold_in(key_of[4], 71), 0),
        "values": gaussian(key_of[2], (PACKED_TOKENS, KEY_HEADS, HEAD_WIDTH), 1.0, 6.0, ((0, 64), (1, 4))),
        "doc_lengths": uneven(key_of[3], DOCS, PACKED_TOKENS, DOC_MOST, 2).astype(jnp.int32),
    }


def reference(queries, keys, values, doc_lengths):
    token_count = queries.shape[0]
    offsets = (jnp.cumsum(doc_lengths) - doc_lengths).astype(jnp.int32)
    padding = REACH * LOCAL_TOKENS
    window_len = padding + LOCAL_TOKENS
    keys_padded = jnp.pad(keys, ((padding, 0), (0, 0), (0, 0)))
    values_padded = jnp.pad(values, ((padding, 0), (0, 0), (0, 0)))
    score_scale = 1.0 / math.sqrt(HEAD_WIDTH)

    def attend_block(block_index):
        query_first = (block_index * LOCAL_TOKENS).astype(jnp.int32)
        query_matrix = lax.dynamic_slice_in_dim(queries, query_first, LOCAL_TOKENS, 0).astype(jnp.float32)
        key_rows = lax.dynamic_slice_in_dim(keys_padded, query_first, window_len, 0).astype(jnp.float32)
        value_rows = lax.dynamic_slice_in_dim(values_padded, query_first, window_len, 0).astype(jnp.float32)
        query_pos = query_first + jnp.arange(LOCAL_TOKENS, dtype=jnp.int32)
        key_pos = query_first - padding + jnp.arange(window_len, dtype=jnp.int32)
        doc_start = lax.optimization_barrier(jnp.max(jnp.where(offsets[None, :] <= query_pos[:, None], offsets[None, :], 0), axis=1))
        allowed = (key_pos[None, :] <= query_pos[:, None]) & (key_pos[None, :] >= doc_start[:, None])
        grouped_heads = query_matrix.reshape(LOCAL_TOKENS, KEY_HEADS, QUERY_PER_KEY, HEAD_WIDTH)
        scores = jnp.einsum('qgjd,kgd->gjqk', grouped_heads, key_rows) * score_scale
        scores = jnp.where(allowed[None, None], scores, -jnp.inf)
        row_max = lax.optimization_barrier(jnp.max(scores, axis=-1, keepdims=True))
        weights = jnp.exp(scores - row_max)
        denom_sum = lax.optimization_barrier(jnp.sum(weights, axis=-1))
        rounded = lax.optimization_barrier(weights.astype(jnp.bfloat16)).astype(jnp.float32)
        mixed = jnp.einsum('gjqk,kgd->qgjd', rounded, value_rows)
        mixed = mixed / jnp.transpose(denom_sum, (2, 0, 1))[..., None]
        return mixed.reshape(LOCAL_TOKENS, HQ, HEAD_WIDTH).astype(jnp.bfloat16)
    attended = lax.map(attend_block, jnp.arange(token_count // LOCAL_TOKENS, dtype=jnp.int32))
    return attended.reshape(token_count, HQ, HEAD_WIDTH)
```

```python
import functools
import math

import jax
import jax.numpy as jnp
from jax import lax
from jax.experimental import pallas as pl
from jax.experimental.pallas import tpu as pltpu
from jax.sharding import PartitionSpec as P

MESH = pl.DeviceIdType.MESH
LAGS = 6
LANES = 128
MASKED = -1e30
TILE = 256


def kernel(
    nc, nh, dl_ref, q_ref, kv_ref, out_ref,
    qe, msk, kvb, acc, mst, obuf, rbuf,
    zs_sem, ss_sem, kr_sem, as_sem, ar_sem,
):
    rows, heads, width = q_ref.shape
    groups = kv_ref.shape[0]
    per = heads // groups
    docs = dl_ref.shape[0]
    part = rows // nh
    tokens = TILE // per
    scale = math.log2(math.e) / math.sqrt(width)
    me = lax.axis_index("ctx")
    mh = lax.axis_index("head")
    core = lax.rem(me, 2)
    sib = me + 1 - 2 * core

    def at(by):
        return lax.rem(me + by + nc, nc)

    def head_at(by):
        return lax.rem(mh + by, nh)

    barrier = pltpu.get_barrier_semaphore()

    def greet(dev):
        pl.semaphore_signal(barrier, inc=1, device_id=dev, device_id_type=MESH)

    greet((at(-2), mh))
    greet((sib, mh))
    for by in range(1, nh):
        greet((me, head_at(by)))

    @pl.when(core == 0)
    def _():
        greet((at(-1), mh))

    pl.semaphore_wait(barrier, nh + 1 + core)

    def source(g, lag):
        return kv_ref.at[g] if lag == 0 else kvb.at[g, lag - 1]

    def along(g, lag):
        return pltpu.make_async_remote_copy(
            src_ref=source(g, lag), dst_ref=kvb.at[g, lag + 1],
            send_sem=zs_sem.at[g, lag // 2], recv_sem=kr_sem.at[g, lag + 1],
            device_id=(at(2), mh), device_id_type=MESH)

    def across(g):
        return pltpu.make_async_remote_copy(
            src_ref=source(g, 4), dst_ref=kvb.at[g, 4],
            send_sem=zs_sem.at[g, 2], recv_sem=kr_sem.at[g, 4],
            device_id=(at(1), mh), device_id_type=MESH)

    def beside(g, lag):
        there = lag - 2 * core
        return pltpu.make_async_remote_copy(
            src_ref=source(g, lag), dst_ref=kvb.at[g, there],
            send_sem=ss_sem.at[g, lag // 2], recv_sem=kr_sem.at[g, there],
            device_id=(sib, mh), device_id_type=MESH)

    def on_core(which, do):
        @pl.when(core == which)
        def _():
            do()

    def arrive(g, lag):
        slot = kvb.at[g, lag - 1]
        pltpu.make_async_remote_copy(
            src_ref=slot, dst_ref=slot, send_sem=zs_sem.at[g, 0], recv_sem=kr_sem.at[g, lag - 1],
            device_id=(sib, mh), device_id_type=MESH).wait_recv()

    for g in range(groups):
        along(g, 0).start()
        on_core(0, lambda g=g: beside(g, 0).start())

    lane = lax.broadcasted_iota(jnp.int32, (8, LANES), 1)
    starts = jnp.full((8, LANES), 1 << 30, jnp.int32)
    ends = jnp.zeros((8, LANES), jnp.int32)
    total = jnp.int32(0)
    for d in range(docs):
        upto = total + dl_ref[d]
        starts = jnp.where(lane == d, total, starts)
        ends = jnp.where(lane == d, upto, ends)
        total = upto
    starts, ends = starts[0:1], ends[0:1]

    for lag in range(LAGS):
        pos = (me - lag) * rows + lax.broadcasted_iota(jnp.int32, (rows, LANES), 0)
        inside = (pos >= starts) & (pos < ends)
        msk[lag] = jnp.where(inside, 0.0, MASKED).astype(jnp.bfloat16)

    def gather_queries(r, _):
        first = pl.multiple_of(r * tokens, tokens)
        at_row = pl.multiple_of(r * TILE, TILE)
        x = q_ref[pl.ds(first, tokens)].astype(jnp.float32)
        pos = me * rows + first + lax.broadcasted_iota(jnp.int32, (tokens, per, LANES), 0)
        inside = (pos >= starts[None]) & (pos < ends[None])
        hot = jnp.where(inside, 1.0, 0.0).reshape(TILE, LANES).astype(jnp.bfloat16)
        for g in range(groups):
            qg = x[:, g * per:(g + 1) * per, :].reshape(TILE, width).astype(jnp.bfloat16)
            qe[g, pl.ds(at_row, TILE), 0:width] = qg
            qe[g, pl.ds(at_row, TILE), width:2 * width] = hot
        return 0

    lax.fori_loop(0, rows // tokens, gather_queries, 0)

    ones = jnp.ones((rows, width), jnp.bfloat16)

    def attend(g, r, lags, first, last):
        at_row = pl.multiple_of(r * TILE, TILE)
        q = qe[g, pl.ds(at_row, TILE), :]
        scores = []
        for lag in lags:
            ref = source(g, lag)
            k = jnp.concatenate([ref[0], msk[lag]], axis=1)
            s = lax.dot_general(q, k, (((1,), (1,)), ((), ())), preferred_element_type=jnp.float32)
            if lag == 0:
                tok = r * tokens + lax.broadcasted_iota(jnp.int32, (tokens, per, rows), 0)
                key = lax.broadcasted_iota(jnp.int32, (tokens, per, rows), 2)
                s = jnp.where(key <= tok, s.reshape(tokens, per, rows), MASKED).reshape(TILE, rows)
            scores.append(s)
        top = functools.reduce(jnp.maximum, scores)
        top = jnp.max(top, axis=1, keepdims=True)
        if not first:
            before = mst[g, pl.ds(at_row, TILE), :]
            top = jnp.maximum(before, top)
        else:
            top = jnp.broadcast_to(top, (TILE, LANES))
        low = top * scale
        low2 = jnp.concatenate([low] * (rows // LANES), axis=1)
        mixed = None
        for lag, s in zip(lags, scores):
            w = jnp.exp2(s * scale - low2).astype(jnp.bfloat16)
            v = jnp.concatenate([source(g, lag)[1], ones], axis=1)
            out = jnp.dot(w, v, preferred_element_type=jnp.float32)
            mixed = out if mixed is None else mixed + out
        if not first:
            fade = jnp.exp2(before * scale - low)
            mixed = mixed + acc[g, pl.ds(at_row, TILE), :] * jnp.concatenate([fade, fade], axis=1)
        if not last:
            mst[g, pl.ds(at_row, TILE), :] = top
            acc[g, pl.ds(at_row, TILE), :] = mixed
            return None
        return (mixed[:, :width] / mixed[:, width:]).astype(jnp.bfloat16)

    def sweep(g, lags, first):
        def body(r, _):
            attend(g, r, lags, first, False)
            return 0
        lax.fori_loop(0, rows * per // TILE, body, 0)

    def give(g, to):
        return pltpu.make_async_remote_copy(
            src_ref=obuf.at[g, to], dst_ref=rbuf.at[g, mh],
            send_sem=as_sem.at[g, to], recv_sem=ar_sem.at[g, mh],
            device_id=(me, to), device_id_type=MESH)

    per_part = part * per // TILE

    def finish(g, lags):
        def chunk(k, _):
            to = head_at(k + 1)

            def body(r, _):
                done = attend(g, to * per_part + r, lags, False, True)
                obuf[g, to, pl.ds(pl.multiple_of(r * TILE, TILE), TILE), :] = done
                return 0
            lax.fori_loop(0, per_part, body, 0)

            @pl.when(k < nh - 1)
            def _():
                give(g, to).start()
            return 0
        lax.fori_loop(0, nh, chunk, 0)

    for g in range(groups):
        sweep(g, (0,), True)

    def forward(g, lag):
        arrive(g, lag)
        if lag == 2:
            along(g, 2).start()
        else:
            on_core(1, across(g).start)
        beside(g, lag).start()

    forward(0, 2)
    arrive(0, 1)
    sweep(0, (1, 2), False)
    forward(0, 4)
    forward(1, 2)
    arrive(0, 3)
    arrive(0, 5)
    finish(0, (3, 4, 5))
    arrive(1, 1)
    sweep(1, (1, 2), False)
    forward(1, 4)
    arrive(1, 3)
    arrive(1, 5)
    finish(1, (3, 4, 5))

    for by in range(1, nh):
        frm = head_at(by)
        for g in range(groups):
            slot = rbuf.at[g, frm]
            pltpu.make_async_remote_copy(
                src_ref=slot, dst_ref=slot, send_sem=as_sem.at[g, frm], recv_sem=ar_sem.at[g, frm],
                device_id=(me, frm), device_id_type=MESH).wait_recv()

    def place(ref_of, frm):
        halves = [ref_of(g)[...].astype(jnp.float32).reshape(part, per, width) for g in range(groups)]
        out_ref[:, pl.ds(pl.multiple_of(frm * heads, heads), heads), :] = jnp.concatenate(halves, axis=1).astype(jnp.bfloat16)

    for by in range(1, nh):
        frm = head_at(by)
        place(lambda g: rbuf.at[g, frm], frm)
    place(lambda g: obuf.at[g, mh], mh)

    for g in range(groups):
        for lag in (0, 2):
            along(g, lag).wait_send()
        on_core(1, across(g).wait_send)
        on_core(0, beside(g, 0).wait_send)
        beside(g, 2).wait_send()
        beside(g, 4).wait_send()
        for by in range(1, nh):
            give(g, head_at(by)).wait_send()


def local(nc, nh, queries, keys, values, doc_lengths):
    rows, heads, width = queries.shape
    groups = keys.shape[1]
    per = heads // groups
    part = rows // nh
    kv = jnp.transpose(jnp.stack((keys, values)), (2, 0, 1, 3))
    bf, f32 = jnp.bfloat16, jnp.float32
    vmem = pl.BlockSpec(memory_space=pltpu.VMEM)
    return pl.pallas_call(
        functools.partial(kernel, nc, nh),
        out_shape=jax.ShapeDtypeStruct((part, heads * nh, width), bf),
        in_specs=[pl.BlockSpec(memory_space=pltpu.SMEM), vmem, vmem],
        out_specs=vmem,
        scratch_shapes=[
            pltpu.VMEM((groups, rows * per, 2 * width), bf),
            pltpu.VMEM((LAGS, rows, LANES), bf),
            pltpu.VMEM((groups, LAGS - 1, 2, rows, width), bf),
            pltpu.VMEM((groups, rows * per, 2 * width), f32),
            pltpu.VMEM((groups, rows * per, LANES), f32),
            pltpu.VMEM((groups, nh, part * per, width), bf),
            pltpu.VMEM((groups, nh, part * per, width), bf),
            pltpu.SemaphoreType.DMA((groups, 3)),
            pltpu.SemaphoreType.DMA((groups, 3)),
            pltpu.SemaphoreType.DMA((groups, LAGS - 1)),
            pltpu.SemaphoreType.DMA((groups, nh)),
            pltpu.SemaphoreType.DMA((groups, nh)),
        ],
        compiler_params=pltpu.CompilerParams(
            collective_id=0, has_side_effects=True, vmem_limit_bytes=48 * 2**20),
        name="attend",
    )(doc_lengths, queries, kv)


def solution(mesh):
    nc, nh = mesh.shape["ctx"], mesh.shape["head"]
    in_specs = (P("ctx", "head", None), P("ctx", "head", None), P("ctx", "head", None), P())
    out_specs = P(("ctx", "head"), None, None)
    return jax.shard_map(
        functools.partial(local, nc, nh), mesh=mesh, in_specs=in_specs, out_specs=out_specs, check_vma=False)
```

```python
import functools
import math

import jax
import jax.numpy as jnp
from jax import lax
from jax.experimental import pallas as pl
from jax.experimental.pallas import tpu as pltpu
from jax.sharding import PartitionSpec as P

MESH = pl.DeviceIdType.MESH
LAGS = 6
LANES = 128
MASKED = -1e30
TILE = 512


def kernel(
    nc, nh, dl_hbm, q_hbm, k_hbm, v_hbm, out_ref,
    dl_ref, q_ref, k_ref, v_ref, own, qe, msk, kvb, sbuf, acc, mst, obuf, rbuf,
    in_sem, zs_sem, ss_sem, kr_sem, as_sem, ar_sem,
):
    rows, heads, width = q_ref.shape
    groups = own.shape[0]
    per = heads // groups
    docs = dl_ref.shape[0]
    part = rows // nh
    tokens = TILE // per
    tiles = rows * per // TILE
    scale = math.log2(math.e) / math.sqrt(width)
    me = lax.axis_index("ctx")
    mh = lax.axis_index("head")
    core = lax.rem(me, 2)
    sib = me + 1 - 2 * core

    def head_at(by):
        return lax.rem(mh + by, nh)

    fetch = [
        pltpu.make_async_copy(src, dst, in_sem.at[n])
        for n, (src, dst) in enumerate(((k_hbm, k_ref), (v_hbm, v_ref), (q_hbm, q_ref), (dl_hbm, dl_ref)))
    ]
    for copy in fetch:
        copy.start()

    barrier = pltpu.get_barrier_semaphore()

    def greet(dev):
        pl.semaphore_signal(barrier, inc=1, device_id=dev, device_id_type=MESH)

    has_next = me + 2 < nc
    crosses = (core == 1) & (me >= 4) & (me + 1 < nc)

    @pl.when(me >= 2)
    def _():
        greet((me - 2, mh))

    @pl.when((core == 0) & (me >= 5))
    def _():
        greet((me - 1, mh))

    greet((sib, mh))
    for by in range(1, nh):
        greet((me, head_at(by)))

    def source(g, lag):
        return own.at[g] if lag == 0 else kvb.at[g, lag - 1]

    def along(g, lag, p):
        return pltpu.make_async_remote_copy(
            src_ref=source(g, lag).at[p], dst_ref=kvb.at[g, lag + 1, p],
            send_sem=zs_sem.at[g, lag // 2, p], recv_sem=kr_sem.at[g, lag + 1, p],
            device_id=(me + 2, mh), device_id_type=MESH)

    def across(g, p):
        return pltpu.make_async_remote_copy(
            src_ref=kvb.at[g, 3, p], dst_ref=kvb.at[g, 4, p],
            send_sem=zs_sem.at[g, 2, p], recv_sem=kr_sem.at[g, 4, p],
            device_id=(me + 1, mh), device_id_type=MESH)

    def beside(g, lag, p):
        there = lag - 2 * core
        return pltpu.make_async_remote_copy(
            src_ref=source(g, lag).at[p], dst_ref=kvb.at[g, there, p],
            send_sem=ss_sem.at[g, lag // 2, p], recv_sem=kr_sem.at[g, there, p],
            device_id=(sib, mh), device_id_type=MESH)

    def arrive(g, lag, p):
        slot = kvb.at[g, lag - 1, p]
        pltpu.make_async_remote_copy(
            src_ref=slot, dst_ref=slot, send_sem=zs_sem.at[g, 0, p], recv_sem=kr_sem.at[g, lag - 1, p],
            device_id=(sib, mh), device_id_type=MESH).wait_recv()

    def send_own(g, p):
        @pl.when(has_next)
        def _():
            along(g, 0, p).start()

        @pl.when(core == 0)
        def _():
            beside(g, 0, p).start()

    def forward(g, lag, p):
        @pl.when(me >= lag)
        def _():
            arrive(g, lag, p)
            if lag == 2:
                @pl.when(has_next)
                def _():
                    along(g, 2, p).start()
            else:
                @pl.when(crosses)
                def _():
                    across(g, p).start()
            beside(g, lag, p).start()

    def await_lag(g, lag):
        @pl.when(me >= lag)
        def _():
            for p in range(2):
                arrive(g, lag, p)

    fetch[3].wait()

    lane = lax.broadcasted_iota(jnp.int32, (8, LANES), 1)
    starts = jnp.full((8, LANES), 1 << 30, jnp.int32)
    ends = jnp.zeros((8, LANES), jnp.int32)
    total = jnp.int32(0)
    for d in range(docs):
        upto = total + dl_ref[d]
        starts = jnp.where(lane == d, total, starts)
        ends = jnp.where(lane == d, upto, ends)
        total = upto
    starts, ends = starts[0:1], ends[0:1]

    pick_row = lax.broadcasted_iota(jnp.int32, (groups * LANES, groups * LANES), 0)
    pick_col = lax.broadcasted_iota(jnp.int32, (groups * LANES, groups * LANES), 1)
    pick = jnp.where(pick_col == lax.rem(pick_row, LANES) * groups + pick_row // LANES, 1.0, 0.0).astype(jnp.bfloat16)
    fetch[0].wait()
    fetch[1].wait()
    for c in range(rows // LANES):
        at_row = c * LANES
        both = [
            jnp.dot(pick, ref[c * groups * LANES:(c + 1) * groups * LANES, :], preferred_element_type=jnp.float32)
            for ref in (k_ref, v_ref)
        ]
        for g in range(groups):
            own[g, 0, at_row:at_row + LANES, :] = both[0][g * LANES:(g + 1) * LANES].astype(jnp.bfloat16)
            own[g, 1, at_row:at_row + LANES, :] = jnp.transpose(both[1][g * LANES:(g + 1) * LANES]).astype(jnp.bfloat16)

    for lag in range(LAGS):
        pos = (me - lag) * rows + lax.broadcasted_iota(jnp.int32, (rows, LANES), 0)
        inside = (pos >= starts) & (pos < ends)
        msk[lag] = jnp.where(inside, 0.0, MASKED).astype(jnp.bfloat16)

    for lag in range(1, LAGS):
        @pl.when(me < lag)
        def _():
            kvb[:, lag - 1] = jnp.zeros((groups, 2, rows, width), jnp.bfloat16)

    pl.semaphore_wait(barrier, nh + has_next.astype(jnp.int32) + crosses.astype(jnp.int32))

    for p in range(2):
        send_own(0, p)

    fetch[2].wait()

    def gather_queries(r, _):
        first = pl.multiple_of(r * tokens, tokens)
        at_row = pl.multiple_of(r * TILE, TILE)
        x = q_ref[pl.ds(first, tokens)].astype(jnp.float32)
        pos = me * rows + first + lax.broadcasted_iota(jnp.int32, (tokens, per, LANES), 0)
        inside = (pos >= starts[None]) & (pos < ends[None])
        hot = jnp.where(inside, 1.0, 0.0).reshape(TILE, LANES).astype(jnp.bfloat16)
        for g in range(groups):
            qg = x[:, g * per:(g + 1) * per, :].reshape(TILE, width).astype(jnp.bfloat16)
            qe[g, pl.ds(at_row, TILE), 0:width] = qg
            qe[g, pl.ds(at_row, TILE), width:2 * width] = hot
        return 0

    lax.fori_loop(0, tiles, gather_queries, 0)

    ones = jnp.ones((16, rows), jnp.bfloat16)

    def score(g, r, lags, slot):
        q = qe[g, pl.ds(pl.multiple_of(r * TILE, TILE), TILE), :]
        top = None
        for n, lag in enumerate(lags):
            k = jnp.concatenate([source(g, lag)[0], msk[lag]], axis=1)
            s = lax.dot_general(k, q, (((1,), (1,)), ((), ())), preferred_element_type=jnp.float32)
            if lag == 0:
                key = lax.broadcasted_iota(jnp.int32, (rows, TILE), 0)
                tok = r * tokens + lax.broadcasted_iota(jnp.int32, (rows, TILE), 1) // per
                s = jnp.where(key <= tok, s, MASKED)
            sbuf[slot, n] = s
            high = jnp.max(s, axis=0, keepdims=True)
            top = high if top is None else jnp.maximum(top, high)
        return top

    def weigh(g, r, lags, slot, top, first, last):
        if not first:
            before = mst[g, r, 0:1, :]
            top = jnp.maximum(before, top)
        low = top * scale
        mixed = None
        for n, lag in enumerate(lags):
            w = jnp.exp2(sbuf[slot, n] * scale - low).astype(jnp.bfloat16)
            vt = source(g, lag)[1]
            vt = jnp.concatenate([vt[:LANES], vt[LANES:]], axis=1)
            vt = jnp.concatenate([vt, ones], axis=0)
            out = jnp.dot(vt, w, preferred_element_type=jnp.float32)
            mixed = out if mixed is None else mixed + out
        if not first:
            fade = jnp.exp2(before * scale - low)
            mixed = mixed + acc[g, r] * fade
        if not last:
            mst[g, r] = jnp.broadcast_to(top, (8, TILE))
            acc[g, r] = mixed
            return None
        return jnp.transpose(mixed[:width] * (1.0 / mixed[width:width + 1])).astype(jnp.bfloat16)

    def sweep(g, lags, order, first, emit=None):
        top = score(g, order[0], lags, 0)
        for t, r in enumerate(order):
            if t + 1 < len(order):
                following = score(g, order[t + 1], lags, (t + 1) % 2)
            done = weigh(g, r, lags, t % 2, top, first, emit is not None)
            if emit is not None:
                emit(t, done)
            top = following

    def give(g, to):
        return pltpu.make_async_remote_copy(
            src_ref=obuf.at[g, to], dst_ref=rbuf.at[g, mh],
            send_sem=as_sem.at[g, to], recv_sem=ar_sem.at[g, mh],
            device_id=(me, to), device_id_type=MESH)

    everywhere = list(range(tiles))
    dests = [head_at(by) for by in (2, 1, 3, 0)]

    def first_sweep(g, _):
        sweep(g, (0,), everywhere, True)
        return 0

    lax.fori_loop(0, groups, first_sweep, 0)
    forward(0, 2, 0)

    def rest(g, _):
        def emit(t, done):
            obuf[g, dests[t]] = done
            if t < nh - 1:
                give(g, dests[t]).start()

        forward(g, 2, 1)

        @pl.when(g == 0)
        def _():
            send_own(1, 0)

            @pl.when(core == 0)
            def _():
                send_own(1, 1)

        await_lag(g, 1)
        sweep(g, (1, 2), everywhere, False)
        forward(g, 4, 0)
        forward(g, 4, 1)

        @pl.when((g == 0) & (core == 1))
        def _():
            send_own(1, 1)

        await_lag(g, 3)
        sweep(g, (3, 4), everywhere, False)

        @pl.when(g == 0)
        def _():
            forward(1, 2, 0)

        await_lag(g, 5)
        sweep(g, (5,), dests, False, emit)
        return 0

    lax.fori_loop(0, groups, rest, 0)

    def place(refs, frm):
        halves = [ref[...].astype(jnp.float32).reshape(part, per, width) for ref in refs]
        out_ref[:, pl.ds(pl.multiple_of(frm * heads, heads), heads), :] = jnp.concatenate(halves, axis=1).astype(jnp.bfloat16)

    place([obuf.at[g, mh] for g in range(groups)], mh)
    for by in (3, 1, 2):
        frm = head_at(by)
        for g in range(groups):
            slot = rbuf.at[g, frm]
            pltpu.make_async_remote_copy(
                src_ref=slot, dst_ref=slot, send_sem=as_sem.at[g, frm], recv_sem=ar_sem.at[g, frm],
                device_id=(me, frm), device_id_type=MESH).wait_recv()
        place([rbuf.at[g, frm] for g in range(groups)], frm)

    def settle(g, _):
        for p in range(2):
            @pl.when(has_next)
            def _():
                along(g, 0, p).wait_send()

            @pl.when(has_next & (me >= 2))
            def _():
                along(g, 2, p).wait_send()

            @pl.when(crosses)
            def _():
                across(g, p).wait_send()

            @pl.when(core == 0)
            def _():
                beside(g, 0, p).wait_send()

            for lag in (2, 4):
                @pl.when(me >= lag)
                def _():
                    beside(g, lag, p).wait_send()
        for by in range(1, nh):
            give(g, head_at(by)).wait_send()
        return 0

    lax.fori_loop(0, groups, settle, 0)


def local(nc, nh, queries, keys, values, doc_lengths):
    rows, heads, width = queries.shape
    groups = keys.shape[1]
    per = heads // groups
    part = rows // nh
    tiles = rows * per // TILE
    bf, f32 = jnp.bfloat16, jnp.float32
    anywhere = pl.BlockSpec(memory_space=pl.ANY)
    return pl.pallas_call(
        functools.partial(kernel, nc, nh),
        out_shape=jax.ShapeDtypeStruct((part, heads * nh, width), bf),
        in_specs=[anywhere, anywhere, anywhere, anywhere],
        out_specs=pl.BlockSpec(memory_space=pltpu.VMEM),
        scratch_shapes=[
            pltpu.SMEM(doc_lengths.shape, jnp.int32),
            pltpu.VMEM((rows, heads, width), bf),
            pltpu.VMEM((rows * groups, width), bf),
            pltpu.VMEM((rows * groups, width), bf),
            pltpu.VMEM((groups, 2, rows, width), bf),
            pltpu.VMEM((groups, rows * per, 2 * width), bf),
            pltpu.VMEM((LAGS, rows, LANES), bf),
            pltpu.VMEM((groups, LAGS - 1, 2, rows, width), bf),
            pltpu.VMEM((2, 2, rows, TILE), f32),
            pltpu.VMEM((groups, tiles, width + 16, TILE), f32),
            pltpu.VMEM((groups, tiles, 8, TILE), f32),
            pltpu.VMEM((groups, nh, part * per, width), bf),
            pltpu.VMEM((groups, nh, part * per, width), bf),
            pltpu.SemaphoreType.DMA((4,)),
            pltpu.SemaphoreType.DMA((groups, 3, 2)),
            pltpu.SemaphoreType.DMA((groups, 3, 2)),
            pltpu.SemaphoreType.DMA((groups, LAGS - 1, 2)),
            pltpu.SemaphoreType.DMA((groups, nh)),
            pltpu.SemaphoreType.DMA((groups, nh)),
        ],
        compiler_params=pltpu.CompilerParams(
            collective_id=0, has_side_effects=True, vmem_limit_bytes=56 * 2**20),
        name="attend",
    )(doc_lengths, queries, keys.reshape(rows * groups, width), values.reshape(rows * groups, width))


def solution(mesh):
    nc, nh = mesh.shape["ctx"], mesh.shape["head"]
    in_specs = (P("ctx", "head", None), P("ctx", "head", None), P("ctx", "head", None), P())
    out_specs = P(("ctx", "head"), None, None)
    return jax.shard_map(
        functools.partial(local, nc, nh), mesh=mesh, in_specs=in_specs, out_specs=out_specs, check_vma=False)
```

```python
import functools
import math

import jax
import jax.numpy as jnp
from jax import lax
from jax.experimental import pallas as pl
from jax.experimental.pallas import tpu as pltpu
from jax.sharding import PartitionSpec as P

MESH = pl.DeviceIdType.MESH
LAGS = 6
LANES = 128
MASKED = -1e30
TILE = 512
DEEP = 8


def kernel(
    nc, nh, dl_hbm, q_hbm, k_hbm, v_hbm, out_ref,
    dl_ref, q_ref, k_ref, v_ref, own, qe, msk, kvb, sbuf, acc, mst, obuf, rbuf, relay,
    in_sem, re_sem, zs_sem, ss_sem, kr_sem, as_sem, ar_sem,
):
    rows, heads, width = q_ref.shape
    groups = own.shape[0]
    per = heads // groups
    docs = dl_ref.shape[0]
    part = rows // nh
    tokens = TILE // per
    tiles = rows * per // TILE
    scale = math.log2(math.e) / math.sqrt(width)
    me = lax.axis_index("ctx")
    mh = lax.axis_index("head")
    core = lax.rem(me, 2)
    sib = me + 1 - 2 * core

    def head_at(by):
        return lax.rem(mh + by, nh)

    fetch = [
        pltpu.make_async_copy(src, dst, in_sem.at[n])
        for n, (src, dst) in enumerate(((k_hbm, k_ref), (v_hbm, v_ref), (q_hbm, q_ref), (dl_hbm, dl_ref)))
    ]
    for copy in fetch:
        copy.start()

    barrier = pltpu.get_barrier_semaphore()

    def greet(dev):
        pl.semaphore_signal(barrier, inc=1, device_id=dev, device_id_type=MESH)

    has_next = me + 2 < nc
    crosses = (core == 1) & (me >= 4) & (me + 1 < nc)

    z = lax.rem(me // 2, DEEP)
    row_first, row_last = me < 2 * DEEP, me >= nc - 2 * DEEP
    last_chip = (z == DEEP - 1) & jnp.logical_not(row_last)
    lends = ((z == DEEP - 2) | ((z == DEEP - 3) & (core == 1))) & jnp.logical_not(row_last)
    hands = ((z == 3) | ((z == 2) & (core == 1))) & jnp.logical_not(row_first)
    to_hands = 10
    hand_on = jnp.where(z == 3, me - 6, me - 5)
    handed = groups - 1

    @pl.when(me >= 2)
    def _():
        greet((me - 2, mh))

    @pl.when((core == 0) & (me >= 5))
    def _():
        greet((me - 1, mh))

    @pl.when(hands)
    def _():
        greet((me - to_hands, mh))

    @pl.when((z == 0) & jnp.logical_not(row_first))
    def _():
        greet((me + 6, mh))

        @pl.when(core == 0)
        def _():
            greet((me + 5, mh))

    greet((sib, mh))
    for by in range(1, nh):
        greet((me, head_at(by)))

    def source(g, lag):
        return own.at[g] if lag == 0 else kvb.at[g, lag - 1]

    def along(g, lag, p):
        return pltpu.make_async_remote_copy(
            src_ref=source(g, lag).at[p], dst_ref=kvb.at[g, lag + 1, p],
            send_sem=zs_sem.at[g, lag // 2, p], recv_sem=kr_sem.at[g, lag + 1, p],
            device_id=(me + 2, mh), device_id_type=MESH)

    def across(g, p):
        return pltpu.make_async_remote_copy(
            src_ref=kvb.at[g, 3, p], dst_ref=kvb.at[g, 4, p],
            send_sem=zs_sem.at[g, 2, p], recv_sem=kr_sem.at[g, 4, p],
            device_id=(me + 1, mh), device_id_type=MESH)

    def beside(g, lag, p):
        there = lag - 2 * core
        return pltpu.make_async_remote_copy(
            src_ref=source(g, lag).at[p], dst_ref=kvb.at[g, there, p],
            send_sem=ss_sem.at[g, lag // 2, p], recv_sem=kr_sem.at[g, there, p],
            device_id=(sib, mh), device_id_type=MESH)

    def lend(p):
        return pltpu.make_async_remote_copy(
            src_ref=own.at[handed, p], dst_ref=relay.at[p], send_sem=re_sem.at[0, p], recv_sem=re_sem.at[1, p],
            device_id=(me + to_hands, mh), device_id_type=MESH)

    def hand(p):
        slot = jnp.where(z == 3, 3, 4)
        return pltpu.make_async_remote_copy(
            src_ref=relay.at[p], dst_ref=kvb.at[handed, slot, p],
            send_sem=re_sem.at[2, p], recv_sem=kr_sem.at[handed, slot, p],
            device_id=(hand_on, mh), device_id_type=MESH)

    def relayed(p):
        pltpu.make_async_remote_copy(
            src_ref=relay.at[p], dst_ref=relay.at[p], send_sem=re_sem.at[0, p], recv_sem=re_sem.at[1, p],
            device_id=(sib, mh), device_id_type=MESH).wait_recv()

    def arrive(g, lag, p):
        slot = kvb.at[g, lag - 1, p]
        pltpu.make_async_remote_copy(
            src_ref=slot, dst_ref=slot, send_sem=zs_sem.at[g, 0, p], recv_sem=kr_sem.at[g, lag - 1, p],
            device_id=(sib, mh), device_id_type=MESH).wait_recv()

    def send_own(g, p):
        @pl.when(has_next)
        def _():
            along(g, 0, p).start()

        @pl.when(core == 0)
        def _():
            beside(g, 0, p).start()

    def forward(g, lag, p):
        @pl.when(me >= lag)
        def _():
            arrive(g, lag, p)
            if lag == 2:
                @pl.when(has_next & jnp.logical_not(last_chip & (g == handed)))
                def _():
                    along(g, 2, p).start()
            else:
                @pl.when(crosses & jnp.logical_not(last_chip & (g == handed)))
                def _():
                    across(g, p).start()
            beside(g, lag, p).start()

    def await_lag(g, lag):
        @pl.when(me >= lag)
        def _():
            for p in range(2):
                arrive(g, lag, p)

    fetch[3].wait()

    lane = lax.broadcasted_iota(jnp.int32, (8, LANES), 1)
    down = lax.broadcasted_iota(jnp.int32, (docs, LANES), 0)
    starts = jnp.full((8, LANES), 1 << 30, jnp.int32)
    ends = jnp.zeros((8, LANES), jnp.int32)
    down_from = jnp.zeros((docs, LANES), jnp.int32)
    down_to = down_from
    total = jnp.int32(0)
    for d in range(docs):
        upto = total + dl_ref[d]
        starts = jnp.where(lane == d, total, starts)
        ends = jnp.where(lane == d, upto, ends)
        down_from = jnp.where(down == d, total, down_from)
        down_to = jnp.where(down == d, upto, down_to)
        total = upto
    starts, ends = starts[0:1], ends[0:1]

    pick_row = lax.broadcasted_iota(jnp.int32, (groups * LANES, groups * LANES), 0)
    pick_col = lax.broadcasted_iota(jnp.int32, (groups * LANES, groups * LANES), 1)
    pick = jnp.where(pick_col == lax.rem(pick_row, LANES) * groups + pick_row // LANES, 1.0, 0.0).astype(jnp.bfloat16)
    fetch[0].wait()
    fetch[1].wait()
    for c in range(rows // LANES):
        at_row = c * LANES
        both = [
            jnp.dot(pick, ref[c * groups * LANES:(c + 1) * groups * LANES, :], preferred_element_type=jnp.float32)
            for ref in (k_ref, v_ref)
        ]
        for g in range(groups):
            own[g, 0, at_row:at_row + LANES, :] = both[0][g * LANES:(g + 1) * LANES].astype(jnp.bfloat16)
            own[g, 1, at_row:at_row + LANES, :] = jnp.transpose(both[1][g * LANES:(g + 1) * LANES]).astype(jnp.bfloat16)

    for lag in range(LAGS):
        pos = (me - lag) * rows + lax.broadcasted_iota(jnp.int32, (rows, LANES), 0)
        inside = (pos >= starts) & (pos < ends)
        msk[lag] = jnp.where(inside, 0.0, MASKED).astype(jnp.bfloat16)

    for lag in range(1, LAGS):
        @pl.when(me < lag)
        def _():
            kvb[:, lag - 1] = jnp.zeros((groups, 2, rows, width), jnp.bfloat16)

    pl.semaphore_wait(barrier, nh + sum(c.astype(jnp.int32) for c in (has_next, crosses, lends, hands)))

    for p in range(2):
        send_own(0, p)

    @pl.when(lends)
    def _():
        for p in range(2):
            lend(p).start()

    @pl.when(z == 0)
    def _():
        for p in range(2):
            send_own(1, p)

    fetch[2].wait()

    eye_row = lax.broadcasted_iota(jnp.int32, (width, width), 0)
    eye_col = lax.broadcasted_iota(jnp.int32, (width, width), 1)
    eye = jnp.where(eye_row == eye_col, 1.0, 0.0).astype(jnp.bfloat16)
    wide = lambda x: jnp.concatenate([x] * (TILE // LANES), axis=1)
    doc_from, doc_to = wide(down_from), wide(down_to)

    def gather_queries(r, _):
        first = pl.multiple_of(r * tokens, tokens)
        x = q_ref[pl.ds(first, tokens)].astype(jnp.float32)
        pos = me * rows + first + lax.broadcasted_iota(jnp.int32, (docs, TILE), 1) // per
        hot = jnp.where((pos >= doc_from) & (pos < doc_to), 1.0, 0.0).astype(jnp.bfloat16)
        for g in range(groups):
            qg = x[:, g * per:(g + 1) * per, :].reshape(TILE, width).astype(jnp.bfloat16)
            turned = lax.dot_general(eye, qg, (((1,), (1,)), ((), ())), preferred_element_type=jnp.float32)
            qe[g, r, 0:width] = turned.astype(jnp.bfloat16)
            qe[g, r, width:width + docs] = hot
            qe[g, r, width + docs:2 * width] = jnp.zeros((width - docs, TILE), jnp.bfloat16)
        return 0

    lax.fori_loop(0, tiles, gather_queries, 0)

    ones = jnp.ones((16, rows), jnp.bfloat16)

    def score(g, r, lags, slot):
        k = [jnp.concatenate([source(g, lag)[0], msk[lag]], axis=1) for lag in lags]
        k = jnp.concatenate(k, axis=0)
        s = jnp.dot(k, qe[g, r], preferred_element_type=jnp.float32)
        if lags == (0,):
            key = lax.broadcasted_iota(jnp.int32, (rows, TILE), 0)
            tok = r * tokens + lax.broadcasted_iota(jnp.int32, (rows, TILE), 1) // per
            s = jnp.where(key <= tok, s, MASKED)
        sbuf[slot, 0:len(lags) * rows] = s
        return jnp.max(s, axis=0, keepdims=True)

    def weigh(g, lags, slot, low):
        w = jnp.exp2(sbuf[slot, 0:len(lags) * rows] * scale - low).astype(jnp.bfloat16)
        vt = []
        for lag in lags:
            half = source(g, lag)[1]
            vt.append(jnp.concatenate([jnp.concatenate([half[:LANES], half[LANES:]], axis=1), ones], axis=0))
        return jnp.dot(jnp.concatenate(vt, axis=1), w, preferred_element_type=jnp.float32)

    def sweep(g, lags, order, first, emit=None):
        top = score(g, order[0], lags, 0)
        for t, r in enumerate(order):
            if not first:
                before = mst[g, r, 0:1, :]
                top = jnp.maximum(before, top)
            low = top * scale
            if t + 1 < len(order):
                following = score(g, order[t + 1], lags, (t + 1) % 2)
            mixed = weigh(g, lags, t % 2, low)
            if not first:
                mixed = mixed + acc[g, r] * jnp.exp2(before * scale - low)
            if emit is None:
                mst[g, r] = jnp.broadcast_to(top, (8, TILE))
                acc[g, r] = mixed
            else:
                emit(t, jnp.transpose(mixed[:width] * (1.0 / mixed[width:width + 1])).astype(jnp.bfloat16))
            top = following

    def give(g, to):
        return pltpu.make_async_remote_copy(
            src_ref=obuf.at[g, to], dst_ref=rbuf.at[g, mh],
            send_sem=as_sem.at[g, to], recv_sem=ar_sem.at[g, mh],
            device_id=(me, to), device_id_type=MESH)

    everywhere = list(range(tiles))
    dests = [head_at(by) for by in (2, 1, 3, 0)]

    def first_sweep(g, _):
        sweep(g, (0,), everywhere, True)
        return 0

    lax.fori_loop(0, groups, first_sweep, 0)
    forward(0, 2, 0)

    def rest(g, _):
        def emit(t, done):
            obuf[g, dests[t]] = done
            if t < nh - 1:
                give(g, dests[t]).start()

        forward(g, 2, 1)

        @pl.when((g == 0) & (z > 0))
        def _():
            send_own(1, 0)

            @pl.when(core == 0)
            def _():
                send_own(1, 1)

        await_lag(g, 1)
        sweep(g, (1, 2), everywhere, False)
        forward(g, 4, 0)
        forward(g, 4, 1)

        @pl.when(g == 0)
        def _():
            @pl.when((core == 1) & (z > 0))
            def _():
                send_own(1, 1)

            @pl.when(hands)
            def _():
                for p in range(2):
                    relayed(p)
                    hand(p).start()

        await_lag(g, 3)
        sweep(g, (3, 4), everywhere, False)

        @pl.when(g == 0)
        def _():
            forward(1, 2, 0)

        await_lag(g, 5)
        sweep(g, (5,), dests, False, emit)
        return 0

    lax.fori_loop(0, groups, rest, 0)

    def place(refs, frm):
        halves = [ref[...].astype(jnp.float32).reshape(part, per, width) for ref in refs]
        out_ref[:, pl.ds(pl.multiple_of(frm * heads, heads), heads), :] = jnp.concatenate(halves, axis=1).astype(jnp.bfloat16)

    place([obuf.at[g, mh] for g in range(groups)], mh)
    for by in (3, 1, 2):
        frm = head_at(by)
        for g in range(groups):
            slot = rbuf.at[g, frm]
            pltpu.make_async_remote_copy(
                src_ref=slot, dst_ref=slot, send_sem=as_sem.at[g, frm], recv_sem=ar_sem.at[g, frm],
                device_id=(me, frm), device_id_type=MESH).wait_recv()
        place([rbuf.at[g, frm] for g in range(groups)], frm)

    def settle(g, _):
        for p in range(2):
            @pl.when(has_next)
            def _():
                along(g, 0, p).wait_send()

            @pl.when(has_next & (me >= 2) & jnp.logical_not(last_chip & (g == handed)))
            def _():
                along(g, 2, p).wait_send()

            @pl.when(crosses & jnp.logical_not(last_chip & (g == handed)))
            def _():
                across(g, p).wait_send()

            @pl.when(core == 0)
            def _():
                beside(g, 0, p).wait_send()

            for lag in (2, 4):
                @pl.when(me >= lag)
                def _():
                    beside(g, lag, p).wait_send()
        for by in range(1, nh):
            give(g, head_at(by)).wait_send()
        return 0

    lax.fori_loop(0, groups, settle, 0)

    for p in range(2):
        @pl.when(lends)
        def _():
            lend(p).wait_send()

        @pl.when(hands)
        def _():
            hand(p).wait_send()


def local(nc, nh, queries, keys, values, doc_lengths):
    rows, heads, width = queries.shape
    groups = keys.shape[1]
    per = heads // groups
    part = rows // nh
    tiles = rows * per // TILE
    bf, f32 = jnp.bfloat16, jnp.float32
    anywhere = pl.BlockSpec(memory_space=pl.ANY)
    return pl.pallas_call(
        functools.partial(kernel, nc, nh),
        out_shape=pltpu.VMEM((part, heads * nh, width), bf),
        in_specs=[anywhere, anywhere, anywhere, anywhere],
        out_specs=pl.BlockSpec(memory_space=pltpu.VMEM),
        scratch_shapes=[
            pltpu.SMEM(doc_lengths.shape, jnp.int32),
            pltpu.VMEM((rows, heads, width), bf),
            pltpu.VMEM((rows * groups, width), bf),
            pltpu.VMEM((rows * groups, width), bf),
            pltpu.VMEM((groups, 2, rows, width), bf),
            pltpu.VMEM((groups, tiles, 2 * width, TILE), bf),
            pltpu.VMEM((LAGS, rows, LANES), bf),
            pltpu.VMEM((groups, LAGS - 1, 2, rows, width), bf),
            pltpu.VMEM((2, 2 * rows, TILE), f32),
            pltpu.VMEM((groups, tiles, width + 16, TILE), f32),
            pltpu.VMEM((groups, tiles, 8, TILE), f32),
            pltpu.VMEM((groups, nh, part * per, width), bf),
            pltpu.VMEM((groups, nh, part * per, width), bf),
            pltpu.VMEM((2, rows, width), bf),
            pltpu.SemaphoreType.DMA((4,)),
            pltpu.SemaphoreType.DMA((3, 2)),
            pltpu.SemaphoreType.DMA((groups, 3, 2)),
            pltpu.SemaphoreType.DMA((groups, 3, 2)),
            pltpu.SemaphoreType.DMA((groups, LAGS - 1, 2)),
            pltpu.SemaphoreType.DMA((groups, nh)),
            pltpu.SemaphoreType.DMA((groups, nh)),
        ],
        compiler_params=pltpu.CompilerParams(
            collective_id=0, has_side_effects=True, vmem_limit_bytes=53 * 2**20),
        name="attend",
    )(doc_lengths, queries, keys.reshape(rows * groups, width), values.reshape(rows * groups, width))


def solution(mesh):
    nc, nh = mesh.shape["ctx"], mesh.shape["head"]
    in_specs = (P("ctx", "head", None), P("ctx", "head", None), P("ctx", "head", None), P())
    out_specs = P(("ctx", "head"), None, None)
    return jax.shard_map(
        functools.partial(local, nc, nh), mesh=mesh, in_specs=in_specs, out_specs=out_specs, check_vma=False)
```

```python
import functools
import math

import jax
import jax.numpy as jnp
from jax import lax
from jax.experimental import pallas as pl
from jax.experimental.pallas import tpu as pltpu
from jax.sharding import PartitionSpec as P

MESH = pl.DeviceIdType.MESH
LAGS = 6
LANES = 128
MASKED = -1e30
TILE = 512
DEEP = 8


def kernel(
    nc, nh, dl_hbm, q_hbm, k_hbm, v_hbm, out_ref,
    dl_ref, q_ref, k_ref, v_ref, own, qe, msk, kvb, sbuf, acc, mst, obuf, rbuf, relay,
    in_sem, re_sem, zs_sem, ss_sem, kr_sem, as_sem, ar_sem,
):
    rows, heads, width = q_ref.shape
    groups = own.shape[0]
    per = heads // groups
    docs = dl_ref.shape[0]
    part = rows // nh
    tokens = TILE // per
    tiles = rows * per // TILE
    scale = math.log2(math.e) / math.sqrt(width)
    me = lax.axis_index("ctx")
    mh = lax.axis_index("head")
    core = lax.rem(me, 2)
    sib = me + 1 - 2 * core

    def head_at(by):
        return lax.rem(mh + by, nh)

    fetch = [
        pltpu.make_async_copy(src, dst, in_sem.at[n])
        for n, (src, dst) in enumerate(((k_hbm, k_ref), (v_hbm, v_ref), (q_hbm, q_ref), (dl_hbm, dl_ref)))
    ]
    for copy in fetch:
        copy.start()

    barrier = pltpu.get_barrier_semaphore()

    def greet(dev):
        pl.semaphore_signal(barrier, inc=1, device_id=dev, device_id_type=MESH)

    has_next = me + 2 < nc
    crosses = (core == 1) & (me >= 4) & (me + 1 < nc)

    z = lax.rem(me // 2, DEEP)
    row_first, row_last = me < 2 * DEEP, me >= nc - 2 * DEEP
    last_chip = (z == DEEP - 1) & jnp.logical_not(row_last)
    first_chip = (z == 0) & jnp.logical_not(row_first)
    spared = last_chip | first_chip
    lends = ((z == DEEP - 2) | ((z == DEEP - 3) & (core == 1))) & jnp.logical_not(row_last)
    hands_same = (z == 3) & jnp.logical_not(row_first)
    hands_other = ((z == 2) | (z == 3)) & (core == 1) & jnp.logical_not(row_first)
    hands = hands_same | hands_other
    handed = groups - 1

    @pl.when(me >= 2)
    def _():
        greet((me - 2, mh))

    @pl.when((core == 0) & (me >= 5))
    def _():
        greet((me - 1, mh))

    @pl.when(hands)
    def _():
        greet((me - 10, mh))

    @pl.when(first_chip)
    def _():
        greet((me + 6, mh))

    @pl.when((z <= 1) & (core == 0) & jnp.logical_not(row_first))
    def _():
        greet((me + 5, mh))

    greet((sib, mh))
    for by in range(1, nh):
        greet((me, head_at(by)))

    def source(g, lag):
        return own.at[g] if lag == 0 else kvb.at[g, lag - 1]

    def along(g, lag, p):
        return pltpu.make_async_remote_copy(
            src_ref=source(g, lag).at[p], dst_ref=kvb.at[g, lag + 1, p],
            send_sem=zs_sem.at[g, lag // 2, p], recv_sem=kr_sem.at[g, lag + 1, p],
            device_id=(me + 2, mh), device_id_type=MESH)

    def across(g, p):
        return pltpu.make_async_remote_copy(
            src_ref=kvb.at[g, 3, p], dst_ref=kvb.at[g, 4, p],
            send_sem=zs_sem.at[g, 2, p], recv_sem=kr_sem.at[g, 4, p],
            device_id=(me + 1, mh), device_id_type=MESH)

    def beside(g, lag, p):
        there = lag - 2 * core
        return pltpu.make_async_remote_copy(
            src_ref=source(g, lag).at[p], dst_ref=kvb.at[g, there, p],
            send_sem=ss_sem.at[g, lag // 2, p], recv_sem=kr_sem.at[g, there, p],
            device_id=(sib, mh), device_id_type=MESH)

    def lend(p):
        return pltpu.make_async_remote_copy(
            src_ref=own.at[handed, p], dst_ref=relay.at[p], send_sem=re_sem.at[0, p], recv_sem=re_sem.at[1, p],
            device_id=(me + 10, mh), device_id_type=MESH)

    def hand_same(p):
        return pltpu.make_async_remote_copy(
            src_ref=relay.at[p], dst_ref=kvb.at[handed, 3, p], send_sem=re_sem.at[2, p], recv_sem=kr_sem.at[handed, 3, p],
            device_id=(me - 6, mh), device_id_type=MESH)

    def hand_other(p):
        return pltpu.make_async_remote_copy(
            src_ref=relay.at[p], dst_ref=kvb.at[handed, 4, p], send_sem=re_sem.at[3, p], recv_sem=kr_sem.at[handed, 4, p],
            device_id=(me - 5, mh), device_id_type=MESH)

    def relayed(p):
        pltpu.make_async_remote_copy(
            src_ref=relay.at[p], dst_ref=relay.at[p], send_sem=re_sem.at[0, p], recv_sem=re_sem.at[1, p],
            device_id=(sib, mh), device_id_type=MESH).wait_recv()

    def arrive(g, lag, p):
        slot = kvb.at[g, lag - 1, p]
        pltpu.make_async_remote_copy(
            src_ref=slot, dst_ref=slot, send_sem=zs_sem.at[g, 0, p], recv_sem=kr_sem.at[g, lag - 1, p],
            device_id=(sib, mh), device_id_type=MESH).wait_recv()

    def send_own(g, p):
        @pl.when(has_next)
        def _():
            along(g, 0, p).start()

        @pl.when(core == 0)
        def _():
            beside(g, 0, p).start()

    def forward(g, lag, p):
        @pl.when(me >= lag)
        def _():
            arrive(g, lag, p)
            if lag == 2:
                @pl.when(has_next & jnp.logical_not(last_chip & (g == handed)))
                def _():
                    along(g, 2, p).start()
            else:
                @pl.when(crosses & jnp.logical_not(spared & (g == handed)))
                def _():
                    across(g, p).start()
            beside(g, lag, p).start()

    def await_lag(g, lag):
        @pl.when(me >= lag)
        def _():
            for p in range(2):
                arrive(g, lag, p)

    pick_row = lax.broadcasted_iota(jnp.int32, (groups * LANES, groups * LANES), 0)
    pick_col = lax.broadcasted_iota(jnp.int32, (groups * LANES, groups * LANES), 1)
    pick = jnp.where(pick_col == lax.rem(pick_row, LANES) * groups + pick_row // LANES, 1.0, 0.0).astype(jnp.bfloat16)

    def separate(ref, p):
        for c in range(rows // LANES):
            at_row = c * LANES
            both = jnp.dot(pick, ref[c * groups * LANES:(c + 1) * groups * LANES, :], preferred_element_type=jnp.float32)
            for g in range(groups):
                one = both[g * LANES:(g + 1) * LANES]
                own[g, p, at_row:at_row + LANES, :] = (jnp.transpose(one) if p else one).astype(jnp.bfloat16)

    fetch[0].wait()
    separate(k_ref, 0)
    pl.semaphore_wait(barrier, nh + sum(c.astype(jnp.int32) for c in (has_next, crosses, lends, hands_same, hands_other)))

    send_own(0, 0)
    fetch[1].wait()
    separate(v_ref, 1)
    send_own(0, 1)

    @pl.when(lends)
    def _():
        for p in range(2):
            lend(p).start()

    @pl.when(z == 0)
    def _():
        for p in range(2):
            send_own(1, p)

    fetch[3].wait()

    lane = lax.broadcasted_iota(jnp.int32, (8, LANES), 1)
    down = lax.broadcasted_iota(jnp.int32, (docs, LANES), 0)
    starts = jnp.full((8, LANES), 1 << 30, jnp.int32)
    ends = jnp.zeros((8, LANES), jnp.int32)
    down_from = jnp.zeros((docs, LANES), jnp.int32)
    down_to = down_from
    total = jnp.int32(0)
    for d in range(docs):
        upto = total + dl_ref[d]
        starts = jnp.where(lane == d, total, starts)
        ends = jnp.where(lane == d, upto, ends)
        down_from = jnp.where(down == d, total, down_from)
        down_to = jnp.where(down == d, upto, down_to)
        total = upto
    starts, ends = starts[0:1], ends[0:1]

    for lag in range(LAGS):
        pos = (me - lag) * rows + lax.broadcasted_iota(jnp.int32, (rows, LANES), 0)
        inside = (pos >= starts) & (pos < ends)
        msk[lag] = jnp.where(inside, 0.0, MASKED).astype(jnp.bfloat16)

    for lag in range(1, LAGS):
        @pl.when(me < lag)
        def _():
            kvb[:, lag - 1] = jnp.zeros((groups, 2, rows, width), jnp.bfloat16)

    fetch[2].wait()

    eye_row = lax.broadcasted_iota(jnp.int32, (width, width), 0)
    eye_col = lax.broadcasted_iota(jnp.int32, (width, width), 1)
    eye = jnp.where(eye_row == eye_col, 1.0, 0.0).astype(jnp.bfloat16)
    wide = lambda x: jnp.concatenate([x] * (TILE // LANES), axis=1)
    doc_from, doc_to = wide(down_from), wide(down_to)

    def gather_queries(r, _):
        first = pl.multiple_of(r * tokens, tokens)
        x = q_ref[pl.ds(first, tokens)].astype(jnp.float32)
        pos = me * rows + first + lax.broadcasted_iota(jnp.int32, (docs, TILE), 1) // per
        hot = jnp.where((pos >= doc_from) & (pos < doc_to), 1.0, 0.0).astype(jnp.bfloat16)
        for g in range(groups):
            qg = x[:, g * per:(g + 1) * per, :].reshape(TILE, width).astype(jnp.bfloat16)
            turned = lax.dot_general(eye, qg, (((1,), (1,)), ((), ())), preferred_element_type=jnp.float32)
            qe[g, r, 0:width] = turned.astype(jnp.bfloat16)
            qe[g, r, width:width + docs] = hot
            qe[g, r, width + docs:2 * width] = jnp.zeros((width - docs, TILE), jnp.bfloat16)
        return 0

    lax.fori_loop(0, tiles, gather_queries, 0)

    ones = jnp.ones((16, rows), jnp.bfloat16)

    def skip(r, lags):
        return r * tokens if lags == (LAGS - 1,) else 0

    def score(g, r, lags, slot):
        low = skip(r, lags)
        k = [jnp.concatenate([source(g, lag)[0, low:], msk[lag, low:]], axis=1) for lag in lags]
        k = jnp.concatenate(k, axis=0)
        s = jnp.dot(k, qe[g, r], preferred_element_type=jnp.float32)
        if lags == (0,):
            key = lax.broadcasted_iota(jnp.int32, (rows, TILE), 0)
            tok = r * tokens + lax.broadcasted_iota(jnp.int32, (rows, TILE), 1) // per
            s = jnp.where(key <= tok, s, MASKED)
        sbuf[slot, low:len(lags) * rows] = s
        return jnp.max(s, axis=0, keepdims=True)

    def weigh(g, r, lags, slot, low):
        cut = skip(r, lags)
        w = jnp.exp2(sbuf[slot, cut:len(lags) * rows] * scale - low).astype(jnp.bfloat16)
        if cut:
            w = jnp.concatenate([jnp.zeros((cut, TILE), jnp.bfloat16), w], axis=0)
        vt = []
        for lag in lags:
            half = source(g, lag)[1]
            vt.append(jnp.concatenate([jnp.concatenate([half[:LANES], half[LANES:]], axis=1), ones], axis=0))
        return jnp.dot(jnp.concatenate(vt, axis=1), w, preferred_element_type=jnp.float32)

    def sweep(g, lags, order, first, emit=None):
        top = score(g, order[0], lags, 0)
        for t, r in enumerate(order):
            if not first:
                before = mst[g, r, 0:1, :]
                top = jnp.maximum(before, top)
            low = top * scale
            if t + 1 < len(order):
                following = score(g, order[t + 1], lags, (t + 1) % 2)
            mixed = weigh(g, r, lags, t % 2, low)
            if not first:
                mixed = mixed + acc[g, r] * jnp.exp2(before * scale - low)
            if emit is None:
                mst[g, r] = jnp.broadcast_to(top, (8, TILE))
                acc[g, r] = mixed
            else:
                emit(t, jnp.transpose(mixed[:width] * (1.0 / mixed[width:width + 1])).astype(jnp.bfloat16))
            top = following

    def give(g, to):
        return pltpu.make_async_remote_copy(
            src_ref=obuf.at[g, to], dst_ref=rbuf.at[g, mh],
            send_sem=as_sem.at[g, to], recv_sem=ar_sem.at[g, mh],
            device_id=(me, to), device_id_type=MESH)

    everywhere = list(range(tiles))
    dests = [head_at(by) for by in (2, 1, 3, 0)]

    def first_sweep(g, _):
        sweep(g, (0,), everywhere, True)
        return 0

    lax.fori_loop(0, groups, first_sweep, 0)
    forward(0, 2, 0)

    def rest(g, _):
        def emit(t, done):
            obuf[g, t] = done

            @pl.when(mh != t)
            def _():
                give(g, t).start()

        @pl.when((g == 0) | (core == 1) | (z == 0))
        def _():
            forward(g, 2, 1)

        @pl.when((g == 0) & (z > 0))
        def _():
            @pl.when(jnp.logical_not(last_chip & (core == 1)))
            def _():
                send_own(1, 0)

            @pl.when(core == 0)
            def _():
                send_own(1, 1)

        await_lag(g, 1)
        sweep(g, (1, 2), everywhere, False)
        forward(g, 4, 0)
        forward(g, 4, 1)

        @pl.when(g == 0)
        def _():
            @pl.when(last_chip & (core == 1))
            def _():
                send_own(1, 0)

            @pl.when((core == 1) & (z > 0))
            def _():
                send_own(1, 1)

            @pl.when(hands)
            def _():
                for p in range(2):
                    relayed(p)

                    @pl.when(hands_same)
                    def _():
                        hand_same(p).start()

                for p in range(2):
                    @pl.when(hands_other)
                    def _():
                        hand_other(p).start()

        await_lag(g, 3)
        sweep(g, (3, 4), everywhere, False)

        @pl.when(g == 0)
        def _():
            forward(1, 2, 0)

            @pl.when((core == 0) & (z > 0))
            def _():
                forward(1, 2, 1)

        await_lag(g, 5)
        sweep(g, (5,), everywhere, False, emit)
        return 0

    lax.fori_loop(0, groups, rest, 0)

    def place(refs, frm):
        halves = [ref[...].astype(jnp.float32).reshape(part, per, width) for ref in refs]
        out_ref[:, pl.ds(pl.multiple_of(frm * heads, heads), heads), :] = jnp.concatenate(halves, axis=1).astype(jnp.bfloat16)

    place([obuf.at[g, mh] for g in range(groups)], mh)
    for by in (3, 1, 2):
        frm = head_at(by)
        for g in range(groups):
            slot = rbuf.at[g, frm]
            pltpu.make_async_remote_copy(
                src_ref=slot, dst_ref=slot, send_sem=as_sem.at[g, frm], recv_sem=ar_sem.at[g, frm],
                device_id=(me, frm), device_id_type=MESH).wait_recv()
        place([rbuf.at[g, frm] for g in range(groups)], frm)

    def settle(g, _):
        for p in range(2):
            @pl.when(has_next)
            def _():
                along(g, 0, p).wait_send()

            @pl.when(has_next & (me >= 2) & jnp.logical_not(last_chip & (g == handed)))
            def _():
                along(g, 2, p).wait_send()

            @pl.when(crosses & jnp.logical_not(spared & (g == handed)))
            def _():
                across(g, p).wait_send()

            @pl.when(core == 0)
            def _():
                beside(g, 0, p).wait_send()

            for lag in (2, 4):
                @pl.when(me >= lag)
                def _():
                    beside(g, lag, p).wait_send()
        for by in range(1, nh):
            give(g, head_at(by)).wait_send()
        return 0

    lax.fori_loop(0, groups, settle, 0)

    for p in range(2):
        @pl.when(lends)
        def _():
            lend(p).wait_send()

        @pl.when(hands_same)
        def _():
            hand_same(p).wait_send()

        @pl.when(hands_other)
        def _():
            hand_other(p).wait_send()


def local(nc, nh, queries, keys, values, doc_lengths):
    rows, heads, width = queries.shape
    groups = keys.shape[1]
    per = heads // groups
    part = rows // nh
    tiles = rows * per // TILE
    bf, f32 = jnp.bfloat16, jnp.float32
    anywhere = pl.BlockSpec(memory_space=pl.ANY)
    return pl.pallas_call(
        functools.partial(kernel, nc, nh),
        out_shape=pltpu.VMEM((part, heads * nh, width), bf),
        in_specs=[anywhere, anywhere, anywhere, anywhere],
        out_specs=pl.BlockSpec(memory_space=pltpu.VMEM),
        scratch_shapes=[
            pltpu.SMEM(doc_lengths.shape, jnp.int32),
            pltpu.VMEM((rows, heads, width), bf),
            pltpu.VMEM((rows * groups, width), bf),
            pltpu.VMEM((rows * groups, width), bf),
            pltpu.VMEM((groups, 2, rows, width), bf),
            pltpu.VMEM((groups, tiles, 2 * width, TILE), bf),
            pltpu.VMEM((LAGS, rows, LANES), bf),
            pltpu.VMEM((groups, LAGS - 1, 2, rows, width), bf),
            pltpu.VMEM((2, 2 * rows, TILE), f32),
            pltpu.VMEM((groups, tiles, width + 16, TILE), f32),
            pltpu.VMEM((groups, tiles, 8, TILE), f32),
            pltpu.VMEM((groups, nh, part * per, width), bf),
            pltpu.VMEM((groups, nh, part * per, width), bf),
            pltpu.VMEM((2, rows, width), bf),
            pltpu.SemaphoreType.DMA((4,)),
            pltpu.SemaphoreType.DMA((4, 2)),
            pltpu.SemaphoreType.DMA((groups, 3, 2)),
            pltpu.SemaphoreType.DMA((groups, 3, 2)),
            pltpu.SemaphoreType.DMA((groups, LAGS - 1, 2)),
            pltpu.SemaphoreType.DMA((groups, nh)),
            pltpu.SemaphoreType.DMA((groups, nh)),
        ],
        compiler_params=pltpu.CompilerParams(
            collective_id=0, has_side_effects=True, vmem_limit_bytes=53 * 2**20),
        name="attend",
    )(doc_lengths, queries, keys.reshape(rows * groups, width), values.reshape(rows * groups, width))


def solution(mesh):
    nc, nh = mesh.shape["ctx"], mesh.shape["head"]
    in_specs = (P("ctx", "head", None), P("ctx", "head", None), P("ctx", "head", None), P())
    out_specs = P(("ctx", "head"), None, None)
    return jax.shard_map(
        functools.partial(local, nc, nh), mesh=mesh, in_specs=in_specs, out_specs=out_specs, check_vma=False)
```

```python
import functools
import math

import jax
import jax.numpy as jnp
from jax import lax
from jax.experimental import pallas as pl
from jax.experimental.pallas import tpu as pltpu
from jax.sharding import PartitionSpec as P

MESH = pl.DeviceIdType.MESH
LAGS = 6
LANES = 128
MASKED = -1e30
TILE = 512
DEEP = 8


def kernel(
    nc, nh, dl_hbm, q_hbm, k_hbm, v_hbm, out_ref,
    dl_ref, q_ref, k_ref, v_ref, own, qe, msk, kvb, sbuf, acc, mst, obuf, rbuf, relay,
    in_sem, re_sem, zs_sem, ss_sem, kr_sem, as_sem, ar_sem,
):
    rows, heads, width = q_ref.shape
    groups = own.shape[0]
    per = heads // groups
    docs = dl_ref.shape[0]
    part = rows // nh
    tokens = TILE // per
    tiles = rows * per // TILE
    scale = math.log2(math.e) / math.sqrt(width)
    me = lax.axis_index("ctx")
    mh = lax.axis_index("head")
    core = lax.rem(me, 2)
    sib = me + 1 - 2 * core

    def head_at(by):
        return lax.rem(mh + by, nh)

    fetch = [
        pltpu.make_async_copy(src, dst, in_sem.at[n])
        for n, (src, dst) in enumerate(((k_hbm, k_ref), (v_hbm, v_ref), (q_hbm, q_ref), (dl_hbm, dl_ref)))
    ]
    for copy in fetch:
        copy.start()

    barrier = pltpu.get_barrier_semaphore()

    def greet(dev):
        pl.semaphore_signal(barrier, inc=1, device_id=dev, device_id_type=MESH)

    has_next = me + 2 < nc
    crosses = (core == 1) & (me >= 4) & (me + 1 < nc)

    z = lax.rem(me // 2, DEEP)
    row_first, row_last = me < 2 * DEEP, me >= nc - 2 * DEEP
    last_chip = (z == DEEP - 1) & jnp.logical_not(row_last)
    first_chip = (z == 0) & jnp.logical_not(row_first)
    spared = last_chip | first_chip
    lends = ((z == DEEP - 2) | ((z == DEEP - 3) & (core == 1))) & jnp.logical_not(row_last)
    hands_same = (z == 3) & jnp.logical_not(row_first)
    hands_other = ((z == 2) | (z == 3)) & (core == 1) & jnp.logical_not(row_first)
    hands = hands_same | hands_other
    handed = groups - 1

    @pl.when(me >= 2)
    def _():
        greet((me - 2, mh))

    @pl.when((core == 0) & (me >= 5))
    def _():
        greet((me - 1, mh))

    @pl.when(hands)
    def _():
        greet((me - 10, mh))

    @pl.when(first_chip)
    def _():
        greet((me + 6, mh))

    @pl.when((z <= 1) & (core == 0) & jnp.logical_not(row_first))
    def _():
        greet((me + 5, mh))

    greet((sib, mh))
    for by in range(1, nh):
        greet((me, head_at(by)))

    def source(g, lag):
        return own.at[g] if lag == 0 else kvb.at[g, lag - 1]

    def along(g, lag, p):
        return pltpu.make_async_remote_copy(
            src_ref=source(g, lag).at[p], dst_ref=kvb.at[g, lag + 1, p],
            send_sem=zs_sem.at[g, lag // 2, p], recv_sem=kr_sem.at[g, lag + 1, p],
            device_id=(me + 2, mh), device_id_type=MESH)

    def across(g, p):
        return pltpu.make_async_remote_copy(
            src_ref=kvb.at[g, 3, p], dst_ref=kvb.at[g, 4, p],
            send_sem=zs_sem.at[g, 2, p], recv_sem=kr_sem.at[g, 4, p],
            device_id=(me + 1, mh), device_id_type=MESH)

    def beside(g, lag, p):
        there = lag - 2 * core
        return pltpu.make_async_remote_copy(
            src_ref=source(g, lag).at[p], dst_ref=kvb.at[g, there, p],
            send_sem=ss_sem.at[g, lag // 2, p], recv_sem=kr_sem.at[g, there, p],
            device_id=(sib, mh), device_id_type=MESH)

    def lend(p):
        return pltpu.make_async_remote_copy(
            src_ref=own.at[handed, p], dst_ref=relay.at[p], send_sem=re_sem.at[0, p], recv_sem=re_sem.at[1, p],
            device_id=(me + 10, mh), device_id_type=MESH)

    def hand_same(p):
        return pltpu.make_async_remote_copy(
            src_ref=relay.at[p], dst_ref=kvb.at[handed, 3, p], send_sem=re_sem.at[2, p], recv_sem=kr_sem.at[handed, 3, p],
            device_id=(me - 6, mh), device_id_type=MESH)

    def hand_other(p):
        return pltpu.make_async_remote_copy(
            src_ref=relay.at[p], dst_ref=kvb.at[handed, 4, p], send_sem=re_sem.at[3, p], recv_sem=kr_sem.at[handed, 4, p],
            device_id=(me - 5, mh), device_id_type=MESH)

    def relayed(p):
        pltpu.make_async_remote_copy(
            src_ref=relay.at[p], dst_ref=relay.at[p], send_sem=re_sem.at[0, p], recv_sem=re_sem.at[1, p],
            device_id=(sib, mh), device_id_type=MESH).wait_recv()

    def arrive(g, lag, p):
        slot = kvb.at[g, lag - 1, p]
        pltpu.make_async_remote_copy(
            src_ref=slot, dst_ref=slot, send_sem=zs_sem.at[g, 0, p], recv_sem=kr_sem.at[g, lag - 1, p],
            device_id=(sib, mh), device_id_type=MESH).wait_recv()

    def send_own(g, p):
        @pl.when(has_next)
        def _():
            along(g, 0, p).start()

        @pl.when(core == 0)
        def _():
            beside(g, 0, p).start()

    def forward(g, lag, p):
        @pl.when(me >= lag)
        def _():
            arrive(g, lag, p)
            if lag == 2:
                @pl.when(has_next & jnp.logical_not(last_chip & (g == handed)))
                def _():
                    along(g, 2, p).start()
            else:
                @pl.when(crosses & jnp.logical_not(spared & (g == handed)))
                def _():
                    across(g, p).start()
            beside(g, lag, p).start()

    def await_lag(g, lag):
        @pl.when(me >= lag)
        def _():
            for p in range(2):
                arrive(g, lag, p)

    pick_row = lax.broadcasted_iota(jnp.int32, (groups * LANES, groups * LANES), 0)
    pick_col = lax.broadcasted_iota(jnp.int32, (groups * LANES, groups * LANES), 1)
    pick = jnp.where(pick_col == lax.rem(pick_row, LANES) * groups + pick_row // LANES, 1.0, 0.0).astype(jnp.bfloat16)

    def separate(ref, p):
        for c in range(rows // LANES):
            at_row = c * LANES
            both = jnp.dot(pick, ref[c * groups * LANES:(c + 1) * groups * LANES, :], preferred_element_type=jnp.float32)
            for g in range(groups):
                one = both[g * LANES:(g + 1) * LANES]
                own[g, p, at_row:at_row + LANES, :] = (jnp.transpose(one) if p else one).astype(jnp.bfloat16)

    fetch[0].wait()
    separate(k_ref, 0)
    pl.semaphore_wait(barrier, nh + sum(c.astype(jnp.int32) for c in (has_next, crosses, lends, hands_same, hands_other)))

    send_own(0, 0)
    fetch[1].wait()
    separate(v_ref, 1)
    send_own(0, 1)

    @pl.when(lends)
    def _():
        for p in range(2):
            lend(p).start()

    @pl.when(z == 0)
    def _():
        for p in range(2):
            send_own(1, p)

    fetch[3].wait()

    lane = lax.broadcasted_iota(jnp.int32, (8, LANES), 1)
    down = lax.broadcasted_iota(jnp.int32, (docs, LANES), 0)
    starts = jnp.full((8, LANES), 1 << 30, jnp.int32)
    ends = jnp.zeros((8, LANES), jnp.int32)
    down_from = jnp.zeros((docs, LANES), jnp.int32)
    down_to = down_from
    total = jnp.int32(0)
    for d in range(docs):
        upto = total + dl_ref[d]
        starts = jnp.where(lane == d, total, starts)
        ends = jnp.where(lane == d, upto, ends)
        down_from = jnp.where(down == d, total, down_from)
        down_to = jnp.where(down == d, upto, down_to)
        total = upto
    starts, ends = starts[0:1], ends[0:1]

    for lag in range(LAGS):
        pos = (me - lag) * rows + lax.broadcasted_iota(jnp.int32, (rows, LANES), 0)
        inside = (pos >= starts) & (pos < ends)
        msk[lag] = jnp.where(inside, 0.0, MASKED).astype(jnp.bfloat16)

    for lag in range(1, LAGS):
        @pl.when(me < lag)
        def _():
            kvb[:, lag - 1] = jnp.zeros((groups, 2, rows, width), jnp.bfloat16)

    fetch[2].wait()

    eye_row = lax.broadcasted_iota(jnp.int32, (width, width), 0)
    eye_col = lax.broadcasted_iota(jnp.int32, (width, width), 1)
    eye = jnp.where(eye_row == eye_col, 1.0, 0.0).astype(jnp.bfloat16)
    wide = lambda x: jnp.concatenate([x] * (TILE // LANES), axis=1)
    doc_from, doc_to = wide(down_from), wide(down_to)

    def gather_queries(r, _):
        first = pl.multiple_of(r * tokens, tokens)
        x = q_ref[pl.ds(first, tokens)].astype(jnp.float32)
        pos = me * rows + first + lax.broadcasted_iota(jnp.int32, (docs, TILE), 1) // per
        hot = jnp.where((pos >= doc_from) & (pos < doc_to), 1.0, 0.0).astype(jnp.bfloat16)
        for g in range(groups):
            qg = x[:, g * per:(g + 1) * per, :].reshape(TILE, width).astype(jnp.bfloat16)
            turned = lax.dot_general(eye, qg, (((1,), (1,)), ((), ())), preferred_element_type=jnp.float32)
            qe[g, r, 0:width] = turned.astype(jnp.bfloat16)
            qe[g, r, width:width + docs] = hot
            qe[g, r, width + docs:2 * width] = jnp.zeros((width - docs, TILE), jnp.bfloat16)
        return 0

    lax.fori_loop(0, tiles, gather_queries, 0)

    ones = jnp.ones((16, rows), jnp.bfloat16)

    def skip(r, lags):
        return r * tokens if lags == (LAGS - 1,) else 0

    def score(g, r, lags, slot):
        low = skip(r, lags)
        k = [jnp.concatenate([source(g, lag)[0, low:], msk[lag, low:]], axis=1) for lag in lags]
        k = jnp.concatenate(k, axis=0)
        s = jnp.dot(k, qe[g, r], preferred_element_type=jnp.float32)
        if lags == (0,):
            key = lax.broadcasted_iota(jnp.int32, (rows, TILE), 0)
            tok = r * tokens + lax.broadcasted_iota(jnp.int32, (rows, TILE), 1) // per
            s = jnp.where(key <= tok, s, MASKED)
        sbuf[slot, low:len(lags) * rows] = s
        return jnp.max(s, axis=0, keepdims=True)

    def weigh(g, r, lags, slot, low):
        cut = skip(r, lags)
        w = jnp.exp2(sbuf[slot, cut:len(lags) * rows] * scale - low).astype(jnp.bfloat16)
        if cut:
            w = jnp.concatenate([jnp.zeros((cut, TILE), jnp.bfloat16), w], axis=0)
        vt = []
        for lag in lags:
            half = source(g, lag)[1]
            vt.append(jnp.concatenate([jnp.concatenate([half[:LANES], half[LANES:]], axis=1), ones], axis=0))
        return jnp.dot(jnp.concatenate(vt, axis=1), w, preferred_element_type=jnp.float32)

    def sweep(g, lags, order, first, emit=None):
        top = score(g, order[0], lags, 0)
        for t, r in enumerate(order):
            if not first:
                before = mst[g, r, 0:1, :]
                top = jnp.maximum(before, top)
            low = top * scale
            if t + 1 < len(order):
                following = score(g, order[t + 1], lags, (t + 1) % 2)
            mixed = weigh(g, r, lags, t % 2, low)
            if not first:
                mixed = mixed + acc[g, r] * jnp.exp2(before * scale - low)
            if emit is None:
                mst[g, r] = jnp.broadcast_to(top, (8, TILE))
                acc[g, r] = mixed
            else:
                emit(t, jnp.transpose(mixed[:width] * (1.0 / mixed[width:width + 1])).astype(jnp.bfloat16))
            top = following

    def give(g, to):
        return pltpu.make_async_remote_copy(
            src_ref=obuf.at[g, to], dst_ref=rbuf.at[g, mh],
            send_sem=as_sem.at[g, to], recv_sem=ar_sem.at[g, mh],
            device_id=(me, to), device_id_type=MESH)

    everywhere = list(range(tiles))
    dests = [head_at(by) for by in (2, 1, 3, 0)]

    def first_sweep(g, _):
        sweep(g, (0,), everywhere, True)
        return 0

    lax.fori_loop(0, groups, first_sweep, 0)
    forward(0, 2, 0)

    def rest(g, _):
        def emit(t, done):
            obuf[g, t] = done

            @pl.when(mh != t)
            def _():
                give(g, t).start()

        @pl.when((g == 0) | (core == 1) | (z == 0))
        def _():
            forward(g, 2, 1)

        @pl.when((g == 0) & (z > 0))
        def _():
            send_own(1, 0)

            @pl.when(core == 0)
            def _():
                send_own(1, 1)

        await_lag(g, 1)
        sweep(g, (1, 2), everywhere, False)
        forward(g, 4, 0)
        forward(g, 4, 1)

        @pl.when(g == 0)
        def _():
            @pl.when((core == 1) & (z > 0))
            def _():
                send_own(1, 1)

            @pl.when(hands)
            def _():
                for p in range(2):
                    relayed(p)

                    @pl.when(hands_same)
                    def _():
                        hand_same(p).start()

                for p in range(2):
                    @pl.when(hands_other)
                    def _():
                        hand_other(p).start()

        await_lag(g, 3)
        sweep(g, (3, 4), everywhere, False)

        @pl.when(g == 0)
        def _():
            forward(1, 2, 0)

            @pl.when((core == 0) & (z > 0))
            def _():
                forward(1, 2, 1)

        await_lag(g, 5)
        sweep(g, (5,), everywhere, False, emit)
        return 0

    lax.fori_loop(0, groups, rest, 0)

    def settle(g, _):
        for p in range(2):
            @pl.when(has_next)
            def _():
                along(g, 0, p).wait_send()

            @pl.when(has_next & (me >= 2) & jnp.logical_not(last_chip & (g == handed)))
            def _():
                along(g, 2, p).wait_send()

            @pl.when(crosses & jnp.logical_not(spared & (g == handed)))
            def _():
                across(g, p).wait_send()

            @pl.when(core == 0)
            def _():
                beside(g, 0, p).wait_send()

            for lag in (2, 4):
                @pl.when(me >= lag)
                def _():
                    beside(g, lag, p).wait_send()
        return 0

    lax.fori_loop(0, groups, settle, 0)

    for p in range(2):
        @pl.when(lends)
        def _():
            lend(p).wait_send()

        @pl.when(hands_same)
        def _():
            hand_same(p).wait_send()

        @pl.when(hands_other)
        def _():
            hand_other(p).wait_send()

    def place(refs, frm):
        halves = [ref[...].astype(jnp.float32).reshape(part, per, width) for ref in refs]
        out_ref[:, pl.ds(pl.multiple_of(frm * heads, heads), heads), :] = jnp.concatenate(halves, axis=1).astype(jnp.bfloat16)

    place([obuf.at[g, mh] for g in range(groups)], mh)
    for by in (3, 1, 2):
        frm = head_at(by)
        for g in range(groups):
            slot = rbuf.at[g, frm]
            pltpu.make_async_remote_copy(
                src_ref=slot, dst_ref=slot, send_sem=as_sem.at[g, frm], recv_sem=ar_sem.at[g, frm],
                device_id=(me, frm), device_id_type=MESH).wait_recv()
        place([rbuf.at[g, frm] for g in range(groups)], frm)

    for g in range(groups):
        for by in range(1, nh):
            give(g, head_at(by)).wait_send()


def local(nc, nh, queries, keys, values, doc_lengths):
    rows, heads, width = queries.shape
    groups = keys.shape[1]
    per = heads // groups
    part = rows // nh
    tiles = rows * per // TILE
    bf, f32 = jnp.bfloat16, jnp.float32
    anywhere = pl.BlockSpec(memory_space=pl.ANY)
    return pl.pallas_call(
        functools.partial(kernel, nc, nh),
        out_shape=pltpu.VMEM((part, heads * nh, width), bf),
        in_specs=[anywhere, anywhere, anywhere, anywhere],
        out_specs=pl.BlockSpec(memory_space=pltpu.VMEM),
        scratch_shapes=[
            pltpu.SMEM(doc_lengths.shape, jnp.int32),
            pltpu.VMEM((rows, heads, width), bf),
            pltpu.VMEM((rows * groups, width), bf),
            pltpu.VMEM((rows * groups, width), bf),
            pltpu.VMEM((groups, 2, rows, width), bf),
            pltpu.VMEM((groups, tiles, 2 * width, TILE), bf),
            pltpu.VMEM((LAGS, rows, LANES), bf),
            pltpu.VMEM((groups, LAGS - 1, 2, rows, width), bf),
            pltpu.VMEM((2, 2 * rows, TILE), f32),
            pltpu.VMEM((groups, tiles, width + 16, TILE), f32),
            pltpu.VMEM((groups, tiles, 8, TILE), f32),
            pltpu.VMEM((groups, nh, part * per, width), bf),
            pltpu.VMEM((groups, nh, part * per, width), bf),
            pltpu.VMEM((2, rows, width), bf),
            pltpu.SemaphoreType.DMA((4,)),
            pltpu.SemaphoreType.DMA((4, 2)),
            pltpu.SemaphoreType.DMA((groups, 3, 2)),
            pltpu.SemaphoreType.DMA((groups, 3, 2)),
            pltpu.SemaphoreType.DMA((groups, LAGS - 1, 2)),
            pltpu.SemaphoreType.DMA((groups, nh)),
            pltpu.SemaphoreType.DMA((groups, nh)),
        ],
        compiler_params=pltpu.CompilerParams(
            collective_id=0, has_side_effects=True, vmem_limit_bytes=53 * 2**20),
        name="attend",
    )(doc_lengths, queries, keys.reshape(rows * groups, width), values.reshape(rows * groups, width))


def solution(mesh):
    nc, nh = mesh.shape["ctx"], mesh.shape["head"]
    in_specs = (P("ctx", "head", None), P("ctx", "head", None), P("ctx", "head", None), P())
    out_specs = P(("ctx", "head"), None, None)
    return jax.shard_map(
        functools.partial(local, nc, nh), mesh=mesh, in_specs=in_specs, out_specs=out_specs, check_vma=False)
```

```python
import functools
import math

import jax
import jax.numpy as jnp
from jax import lax
from jax.experimental import pallas as pl
from jax.experimental.pallas import tpu as pltpu
from jax.sharding import PartitionSpec as P

MESH = pl.DeviceIdType.MESH
LAGS = 6
LANES = 128
MASKED = -1e30
TILE = 512
DEEP = 8


def kernel(
    nc, nh, dl_hbm, q_hbm, k_hbm, v_hbm, out_ref,
    dl_ref, q_ref, k_ref, v_ref, own, qe, msk, kvb, sbuf, acc, mst, obuf, rbuf, relay,
    in_sem, re_sem, zs_sem, ss_sem, kr_sem, as_sem, ar_sem,
):
    rows, heads, width = q_ref.shape
    groups = own.shape[0]
    per = heads // groups
    docs = dl_ref.shape[0]
    part = rows // nh
    tokens = TILE // per
    tiles = rows * per // TILE
    scale = math.log2(math.e) / math.sqrt(width)
    me = lax.axis_index("ctx")
    mh = lax.axis_index("head")
    core = lax.rem(me, 2)
    sib = me + 1 - 2 * core

    def head_at(by):
        return lax.rem(mh + by, nh)

    fetch = [
        pltpu.make_async_copy(src, dst, in_sem.at[n])
        for n, (src, dst) in enumerate(((k_hbm, k_ref), (v_hbm, v_ref), (q_hbm, q_ref), (dl_hbm, dl_ref)))
    ]
    for copy in fetch:
        copy.start()

    barrier = pltpu.get_barrier_semaphore()

    def greet(dev):
        pl.semaphore_signal(barrier, inc=1, device_id=dev, device_id_type=MESH)

    has_next = me + 2 < nc

    z = lax.rem(me // 2, DEEP)
    row_first, row_last = me < 2 * DEEP, me >= nc - 2 * DEEP
    last_chip = (z == DEEP - 1) & jnp.logical_not(row_last)
    first_chip = (z == 0) & jnp.logical_not(row_first)
    crosses = (core == 1) & (me >= 4) & (me + 1 < nc) & jnp.logical_not(last_chip)
    lends = ((z == DEEP - 2) | ((z == DEEP - 3) & (core == 1))) & jnp.logical_not(row_last)
    hands_same = (z == 3) & jnp.logical_not(row_first)
    hands_other = ((z == 2) | (z == 3)) & (core == 1) & jnp.logical_not(row_first)
    hands = hands_same | hands_other
    lends_both = (z == DEEP - 3) & lends
    hands_both = (z == 2) & hands
    handed = groups - 1

    @pl.when(me >= 2)
    def _():
        greet((me - 2, mh))

    @pl.when((core == 0) & (me >= 5) & jnp.logical_not(first_chip))
    def _():
        greet((me - 1, mh))

    @pl.when(hands)
    def _():
        greet((me - 10, mh))

    @pl.when(first_chip)
    def _():
        greet((me + 6, mh))

    @pl.when((z <= 1) & (core == 0) & jnp.logical_not(row_first))
    def _():
        greet((me + 5, mh))

    greet((sib, mh))
    for by in range(1, nh):
        greet((me, head_at(by)))

    def source(g, lag):
        return own.at[g] if lag == 0 else kvb.at[g, lag - 1]

    def along(g, lag, p):
        return pltpu.make_async_remote_copy(
            src_ref=source(g, lag).at[p], dst_ref=kvb.at[g, lag + 1, p],
            send_sem=zs_sem.at[g, lag // 2, p], recv_sem=kr_sem.at[g, lag + 1, p],
            device_id=(me + 2, mh), device_id_type=MESH)

    def across(g, p):
        return pltpu.make_async_remote_copy(
            src_ref=kvb.at[g, 3, p], dst_ref=kvb.at[g, 4, p],
            send_sem=zs_sem.at[g, 2, p], recv_sem=kr_sem.at[g, 4, p],
            device_id=(me + 1, mh), device_id_type=MESH)

    def beside(g, lag, p):
        there = lag - 2 * core
        return pltpu.make_async_remote_copy(
            src_ref=source(g, lag).at[p], dst_ref=kvb.at[g, there, p],
            send_sem=ss_sem.at[g, lag // 2, p], recv_sem=kr_sem.at[g, there, p],
            device_id=(sib, mh), device_id_type=MESH)

    def lend(g, p):
        return pltpu.make_async_remote_copy(
            src_ref=own.at[g, p], dst_ref=relay.at[g, p], send_sem=re_sem.at[0, g, p], recv_sem=re_sem.at[1, g, p],
            device_id=(me + 10, mh), device_id_type=MESH)

    def hand_same(p):
        return pltpu.make_async_remote_copy(
            src_ref=relay.at[handed, p], dst_ref=kvb.at[handed, 3, p],
            send_sem=re_sem.at[2, handed, p], recv_sem=kr_sem.at[handed, 3, p],
            device_id=(me - 6, mh), device_id_type=MESH)

    def hand_other(g, p):
        return pltpu.make_async_remote_copy(
            src_ref=relay.at[g, p], dst_ref=kvb.at[g, 4, p], send_sem=re_sem.at[3, g, p], recv_sem=kr_sem.at[g, 4, p],
            device_id=(me - 5, mh), device_id_type=MESH)

    def relayed(g, p):
        pltpu.make_async_remote_copy(
            src_ref=relay.at[g, p], dst_ref=relay.at[g, p], send_sem=re_sem.at[0, g, p], recv_sem=re_sem.at[1, g, p],
            device_id=(sib, mh), device_id_type=MESH).wait_recv()

    def arrive(g, lag, p):
        slot = kvb.at[g, lag - 1, p]
        pltpu.make_async_remote_copy(
            src_ref=slot, dst_ref=slot, send_sem=zs_sem.at[g, 0, p], recv_sem=kr_sem.at[g, lag - 1, p],
            device_id=(sib, mh), device_id_type=MESH).wait_recv()

    def send_own(g, p):
        @pl.when(has_next)
        def _():
            along(g, 0, p).start()

        @pl.when(core == 0)
        def _():
            beside(g, 0, p).start()

    def forward(g, lag, p):
        @pl.when(me >= lag)
        def _():
            arrive(g, lag, p)
            if lag == 2:
                @pl.when(has_next & jnp.logical_not(last_chip & (g == handed)))
                def _():
                    along(g, 2, p).start()
            else:
                @pl.when(crosses & jnp.logical_not(first_chip & (g == handed)))
                def _():
                    across(g, p).start()
            beside(g, lag, p).start()

    def await_lag(g, lag):
        @pl.when(me >= lag)
        def _():
            for p in range(2):
                arrive(g, lag, p)

    pick_row = lax.broadcasted_iota(jnp.int32, (groups * LANES, groups * LANES), 0)
    pick_col = lax.broadcasted_iota(jnp.int32, (groups * LANES, groups * LANES), 1)
    pick = jnp.where(pick_col == lax.rem(pick_row, LANES) * groups + pick_row // LANES, 1.0, 0.0).astype(jnp.bfloat16)

    def separate(ref, p):
        for c in range(rows // LANES):
            at_row = c * LANES
            both = jnp.dot(pick, ref[c * groups * LANES:(c + 1) * groups * LANES, :], preferred_element_type=jnp.float32)
            for g in range(groups):
                one = both[g * LANES:(g + 1) * LANES]
                own[g, p, at_row:at_row + LANES, :] = (jnp.transpose(one) if p else one).astype(jnp.bfloat16)

    fetch[0].wait()
    separate(k_ref, 0)
    pl.semaphore_wait(barrier, nh + sum(c.astype(jnp.int32) for c in (has_next, crosses, lends, hands_same, hands_other)))

    send_own(0, 0)
    fetch[1].wait()
    separate(v_ref, 1)
    send_own(0, 1)

    @pl.when(lends_both)
    def _():
        for p in range(2):
            lend(0, p).start()

    @pl.when(lends)
    def _():
        for p in range(2):
            lend(handed, p).start()

    @pl.when(z == 0)
    def _():
        for p in range(2):
            send_own(1, p)

    fetch[3].wait()

    lane = lax.broadcasted_iota(jnp.int32, (8, LANES), 1)
    down = lax.broadcasted_iota(jnp.int32, (docs, LANES), 0)
    starts = jnp.full((8, LANES), 1 << 30, jnp.int32)
    ends = jnp.zeros((8, LANES), jnp.int32)
    down_from = jnp.zeros((docs, LANES), jnp.int32)
    down_to = down_from
    total = jnp.int32(0)
    for d in range(docs):
        upto = total + dl_ref[d]
        starts = jnp.where(lane == d, total, starts)
        ends = jnp.where(lane == d, upto, ends)
        down_from = jnp.where(down == d, total, down_from)
        down_to = jnp.where(down == d, upto, down_to)
        total = upto
    starts, ends = starts[0:1], ends[0:1]

    for lag in range(LAGS):
        pos = (me - lag) * rows + lax.broadcasted_iota(jnp.int32, (rows, LANES), 0)
        inside = (pos >= starts) & (pos < ends)
        msk[lag] = jnp.where(inside, 0.0, MASKED).astype(jnp.bfloat16)

    for lag in range(1, LAGS):
        @pl.when(me < lag)
        def _():
            kvb[:, lag - 1] = jnp.zeros((groups, 2, rows, width), jnp.bfloat16)

    fetch[2].wait()

    eye_row = lax.broadcasted_iota(jnp.int32, (width, width), 0)
    eye_col = lax.broadcasted_iota(jnp.int32, (width, width), 1)
    eye = jnp.where(eye_row == eye_col, 1.0, 0.0).astype(jnp.bfloat16)
    wide = lambda x: jnp.concatenate([x] * (TILE // LANES), axis=1)
    doc_from, doc_to = wide(down_from), wide(down_to)

    def gather_queries(r, _):
        first = pl.multiple_of(r * tokens, tokens)
        x = q_ref[pl.ds(first, tokens)].astype(jnp.float32)
        pos = me * rows + first + lax.broadcasted_iota(jnp.int32, (docs, TILE), 1) // per
        hot = jnp.where((pos >= doc_from) & (pos < doc_to), 1.0, 0.0).astype(jnp.bfloat16)
        for g in range(groups):
            qg = x[:, g * per:(g + 1) * per, :].reshape(TILE, width).astype(jnp.bfloat16)
            turned = lax.dot_general(eye, qg, (((1,), (1,)), ((), ())), preferred_element_type=jnp.float32)
            qe[g, r, 0:width] = turned.astype(jnp.bfloat16)
            qe[g, r, width:width + docs] = hot
            qe[g, r, width + docs:2 * width] = jnp.zeros((width - docs, TILE), jnp.bfloat16)
        return 0

    lax.fori_loop(0, tiles, gather_queries, 0)

    ones = jnp.ones((16, rows), jnp.bfloat16)

    def skip(r, lags):
        return r * tokens if lags == (LAGS - 1,) else 0

    def score(g, r, lags, slot):
        low = skip(r, lags)
        k = [jnp.concatenate([source(g, lag)[0, low:], msk[lag, low:]], axis=1) for lag in lags]
        k = jnp.concatenate(k, axis=0)
        s = jnp.dot(k, qe[g, r], preferred_element_type=jnp.float32)
        if lags == (0,):
            key = lax.broadcasted_iota(jnp.int32, (rows, TILE), 0)
            tok = r * tokens + lax.broadcasted_iota(jnp.int32, (rows, TILE), 1) // per
            s = jnp.where(key <= tok, s, MASKED)
        sbuf[slot, low:len(lags) * rows] = s
        return jnp.max(s, axis=0, keepdims=True)

    def weigh(g, r, lags, slot, low):
        cut = skip(r, lags)
        w = jnp.exp2(sbuf[slot, cut:len(lags) * rows] * scale - low).astype(jnp.bfloat16)
        if cut:
            w = jnp.concatenate([jnp.zeros((cut, TILE), jnp.bfloat16), w], axis=0)
        vt = []
        for lag in lags:
            half = source(g, lag)[1]
            vt.append(jnp.concatenate([jnp.concatenate([half[:LANES], half[LANES:]], axis=1), ones], axis=0))
        return jnp.dot(jnp.concatenate(vt, axis=1), w, preferred_element_type=jnp.float32)

    def sweep(g, lags, order, first, emit=None):
        top = score(g, order[0], lags, 0)
        for t, r in enumerate(order):
            if not first:
                before = mst[g, r, 0:1, :]
                top = jnp.maximum(before, top)
            low = top * scale
            if t + 1 < len(order):
                following = score(g, order[t + 1], lags, (t + 1) % 2)
            mixed = weigh(g, r, lags, t % 2, low)
            if not first:
                mixed = mixed + acc[g, r] * jnp.exp2(before * scale - low)
            if emit is None:
                mst[g, r] = jnp.broadcast_to(top, (8, TILE))
                acc[g, r] = mixed
            else:
                emit(t, jnp.transpose(mixed[:width] * (1.0 / mixed[width:width + 1])).astype(jnp.bfloat16))
            top = following

    def give(g, to):
        return pltpu.make_async_remote_copy(
            src_ref=obuf.at[g, to], dst_ref=rbuf.at[g, mh],
            send_sem=as_sem.at[g, to], recv_sem=ar_sem.at[g, mh],
            device_id=(me, to), device_id_type=MESH)

    everywhere = list(range(tiles))
    dests = [head_at(by) for by in (2, 1, 3, 0)]

    def first_sweep(g, _):
        sweep(g, (0,), everywhere, True)
        return 0

    lax.fori_loop(0, groups, first_sweep, 0)
    forward(0, 2, 0)

    def rest(g, _):
        def emit(t, done):
            obuf[g, t] = done

            @pl.when(mh != t)
            def _():
                give(g, t).start()

        @pl.when((g == 0) | (core == 1) | (z == 0))
        def _():
            forward(g, 2, 1)

        @pl.when((g == 0) & (z > 0))
        def _():
            send_own(1, 0)

            @pl.when(core == 0)
            def _():
                send_own(1, 1)

        await_lag(g, 1)
        sweep(g, (1, 2), everywhere, False)
        forward(g, 4, 0)
        forward(g, 4, 1)

        @pl.when(g == 0)
        def _():
            @pl.when((core == 1) & (z > 0))
            def _():
                send_own(1, 1)

            @pl.when(hands_both)
            def _():
                for p in range(2):
                    relayed(0, p)
                    hand_other(0, p).start()

            @pl.when(hands)
            def _():
                for p in range(2):
                    relayed(handed, p)

                    @pl.when(hands_same)
                    def _():
                        hand_same(p).start()

                for p in range(2):
                    @pl.when(hands_other)
                    def _():
                        hand_other(handed, p).start()

        await_lag(g, 3)
        sweep(g, (3, 4), everywhere, False)

        @pl.when(g == 0)
        def _():
            forward(1, 2, 0)

            @pl.when((core == 0) & (z > 0))
            def _():
                forward(1, 2, 1)

        await_lag(g, 5)
        sweep(g, (5,), everywhere, False, emit)
        return 0

    lax.fori_loop(0, groups, rest, 0)

    def settle(g, _):
        for p in range(2):
            @pl.when(has_next)
            def _():
                along(g, 0, p).wait_send()

            @pl.when(has_next & (me >= 2) & jnp.logical_not(last_chip & (g == handed)))
            def _():
                along(g, 2, p).wait_send()

            @pl.when(crosses & jnp.logical_not(first_chip & (g == handed)))
            def _():
                across(g, p).wait_send()

            @pl.when(core == 0)
            def _():
                beside(g, 0, p).wait_send()

            for lag in (2, 4):
                @pl.when(me >= lag)
                def _():
                    beside(g, lag, p).wait_send()
        return 0

    lax.fori_loop(0, groups, settle, 0)

    for p in range(2):
        @pl.when(lends)
        def _():
            lend(handed, p).wait_send()

        @pl.when(lends_both)
        def _():
            lend(0, p).wait_send()

        @pl.when(hands_same)
        def _():
            hand_same(p).wait_send()

        @pl.when(hands_other)
        def _():
            hand_other(handed, p).wait_send()

        @pl.when(hands_both)
        def _():
            hand_other(0, p).wait_send()

    def place(refs, frm):
        halves = [ref[...].astype(jnp.float32).reshape(part, per, width) for ref in refs]
        out_ref[:, pl.ds(pl.multiple_of(frm * heads, heads), heads), :] = jnp.concatenate(halves, axis=1).astype(jnp.bfloat16)

    place([obuf.at[g, mh] for g in range(groups)], mh)
    for by in (3, 1, 2):
        frm = head_at(by)
        for g in range(groups):
            slot = rbuf.at[g, frm]
            pltpu.make_async_remote_copy(
                src_ref=slot, dst_ref=slot, send_sem=as_sem.at[g, frm], recv_sem=ar_sem.at[g, frm],
                device_id=(me, frm), device_id_type=MESH).wait_recv()
        place([rbuf.at[g, frm] for g in range(groups)], frm)

    for g in range(groups):
        for by in range(1, nh):
            give(g, head_at(by)).wait_send()


def local(nc, nh, queries, keys, values, doc_lengths):
    rows, heads, width = queries.shape
    groups = keys.shape[1]
    per = heads // groups
    part = rows // nh
    tiles = rows * per // TILE
    bf, f32 = jnp.bfloat16, jnp.float32
    anywhere = pl.BlockSpec(memory_space=pl.ANY)
    return pl.pallas_call(
        functools.partial(kernel, nc, nh),
        out_shape=pltpu.VMEM((part, heads * nh, width), bf),
        in_specs=[anywhere, anywhere, anywhere, anywhere],
        out_specs=pl.BlockSpec(memory_space=pltpu.VMEM),
        scratch_shapes=[
            pltpu.SMEM(doc_lengths.shape, jnp.int32),
            pltpu.VMEM((rows, heads, width), bf),
            pltpu.VMEM((rows * groups, width), bf),
            pltpu.VMEM((rows * groups, width), bf),
            pltpu.VMEM((groups, 2, rows, width), bf),
            pltpu.VMEM((groups, tiles, 2 * width, TILE), bf),
            pltpu.VMEM((LAGS, rows, LANES), bf),
            pltpu.VMEM((groups, LAGS - 1, 2, rows, width), bf),
            pltpu.VMEM((2, 2 * rows, TILE), f32),
            pltpu.VMEM((groups, tiles, width + 16, TILE), f32),
            pltpu.VMEM((groups, tiles, 8, TILE), f32),
            pltpu.VMEM((groups, nh, part * per, width), bf),
            pltpu.VMEM((groups, nh, part * per, width), bf),
            pltpu.VMEM((groups, 2, rows, width), bf),
            pltpu.SemaphoreType.DMA((4,)),
            pltpu.SemaphoreType.DMA((4, groups, 2)),
            pltpu.SemaphoreType.DMA((groups, 3, 2)),
            pltpu.SemaphoreType.DMA((groups, 3, 2)),
            pltpu.SemaphoreType.DMA((groups, LAGS - 1, 2)),
            pltpu.SemaphoreType.DMA((groups, nh)),
            pltpu.SemaphoreType.DMA((groups, nh)),
        ],
        compiler_params=pltpu.CompilerParams(
            collective_id=0, has_side_effects=True, vmem_limit_bytes=53 * 2**20),
        name="attend",
    )(doc_lengths, queries, keys.reshape(rows * groups, width), values.reshape(rows * groups, width))


def solution(mesh):
    nc, nh = mesh.shape["ctx"], mesh.shape["head"]
    in_specs = (P("ctx", "head", None), P("ctx", "head", None), P("ctx", "head", None), P())
    out_specs = P(("ctx", "head"), None, None)
    return jax.shard_map(
        functools.partial(local, nc, nh), mesh=mesh, in_specs=in_specs, out_specs=out_specs, check_vma=False)
```
